128 devices in a mesh: surf: 4 (over z_hi, core), shot: 32 (over z_lo, x, y).
Axes of the slice: x: 4, y: 4, z: 4 (z_hi: 2, z_lo: 2; z = z_hi * 2 + z_lo), core: 2. Of those that a mesh axis runs over, the one named last changes fastest.
Arguments:
- traces: bfloat16 [256, 640, 1024], P('shot'), may hold values from -6 to 6
- surface_point: int32 [4, 4, 2], replicated, may hold values from 0 to 639, as said below
- gather_index: int32 [4, 4, 2], replicated, may hold values from 0 to 255, as said below
Outputs:
- prediction: bfloat16 [256, 640, 1024], P('shot', 'surf')
The draws below stay inside these ranges and needn't reach their ends.
Inputs may be any that keep to these rules, and one draw needn't show every extreme that they name: `surface_point`: all 32 entries are distinct. `gather_index`: the 2 entries of one round and group are distinct and lie on one index of shot: they share their quotient by 8.
All inputs are finite; a program needn't handle non-finite values.
Results may differ from the reference program's by a relative error of at most 0.015.
Values may be sent and summed in bfloat16 or wider, within the bound.
A program may use at most 128 MiB of HBM per device.

```python
import math
import jax
import jax.numpy as jnp
from jax import lax

SHOT_DEV = 8
R = 640
NT = 1024
F = 256
KB = 2
ROUNDS = 4
SHOTS = 256
N_SURF = 4
N_SHOT = 32


def draw_surface_point(key, part):
    key = jax.random.fold_in(key, 11)
    point_count = ROUNDS * N_SURF * KB
    middle = jax.random.permutation(key, R - 2)[:point_count - 2] + 1
    chosen = jnp.concatenate([middle.astype(jnp.int32), jnp.array([0, R - 1], dtype=jnp.int32)])
    shuffle = jax.random.permutation(jax.random.fold_in(key, 1), point_count)
    return chosen[shuffle].astype(jnp.int32).reshape(ROUNDS, N_SURF, KB)


def draw_gather_index(key, part):
    key = jax.random.fold_in(key, 23)
    owner_key = jax.random.fold_in(key, 1)
    score_key = jax.random.fold_in(key, 2)
    owners = jax.random.randint(owner_key, (ROUNDS, N_SURF, 1), 0, N_SHOT).astype(jnp.int32)
    owners = owners.at[0, 0, 0].set(0).at[0, N_SURF - 1, 0].set(N_SHOT - 1)
    scores = jax.random.randint(score_key, (ROUNDS, N_SURF, SHOT_DEV), 0, 4096).astype(jnp.int32)
    scores = scores * SHOT_DEV + jnp.arange(SHOT_DEV, dtype=jnp.int32)
    scores = scores.at[0, 0, 0].set(-1).at[0, N_SURF - 1, SHOT_DEV - 1].set(-1)
    local_rows = jnp.argsort(scores, axis=-1, stable=True)[..., :KB].astype(jnp.int32)
    return (owners * SHOT_DEV + local_rows).astype(jnp.int32)


def levels(own_key, shape, split, least, high):
    loudness = 1.0
    for position, parts in split:
        heights = jax.random.uniform(jax.random.fold_in(jax.random.fold_in(own_key, 6), position), (parts,), jnp.float32, least / len(split), high / len(split))
        loudness = loudness * jnp.repeat(jnp.exp(heights), shape[position] // parts).reshape((-1,) + (1,) * (len(shape) - 1 - position))
    return loudness


def scatter_about(rng, shape, width, bound, cuts=(), kind=jnp.bfloat16):
    values = width * jax.random.normal(rng, shape, jnp.float32)
    if cuts:
        values = values * levels(rng, shape, cuts, -0.22, 0.18)
    return jnp.clip(values, -bound, bound).astype(kind)


def setup_inputs(seed: int = 0) -> dict:
    key_list = jax.random.split(jax.random.key(seed), 4)
    traces = scatter_about(key_list[0], (SHOTS, R, NT), 1.0, 6.0, ((0, 32),))
    surface_point = draw_surface_point(jax.random.fold_in(key_list[3], 71), 0)
    gather_index = draw_gather_index(jax.random.fold_in(key_list[3], 71), 0)
    return {"traces": traces, "surface_point": surface_point, "gather_index": gather_index}


def dft_table(samples, freq_bins):
    time_index = jnp.arange(samples, dtype=jnp.int32)[:, None]
    freq_index = jnp.arange(freq_bins, dtype=jnp.int32)[None, :]
    phase_int = (time_index * freq_index) % samples
    angles = phase_int.astype(jnp.float32) * (2.0 * math.pi / samples)
    return jnp.concatenate([jnp.cos(angles), -jnp.sin(angles)], axis=1).astype(jnp.bfloat16)


def spectral_product(near_spec, far_spec, half_bins):
    near_real = near_spec[..., :half_bins].astype(jnp.float32)
    near_imag = near_spec[..., half_bins:].astype(jnp.float32)
    far_real = far_spec[..., :half_bins].astype(jnp.float32)
    far_imag = far_spec[..., half_bins:].astype(jnp.float32)
    left_real = jnp.concatenate([near_real, -near_imag], axis=1)
    right_real = jnp.concatenate([far_real, far_imag], axis=0)
    left_imag = jnp.concatenate([near_real, near_imag], axis=1)
    right_imag = jnp.concatenate([far_imag, far_real], axis=0)
    real_part = jnp.einsum("skf,krf->srf", left_real, right_real)
    imag_part = jnp.einsum("skf,krf->srf", left_imag, right_imag)
    return jnp.concatenate([real_part, imag_part], axis=2)


def reference(traces, surface_point, gather_index):
    shot_total, receivers, samples = traces.shape
    forward = dft_table(samples, F)
    forward_wide = forward.astype(jnp.float32)
    factor = samples ** -0.5
    far_all = []
    for group_index in range(N_SURF):
        wanted = gather_index[:, group_index, :].reshape(-1)
        picked = jnp.take(traces, wanted, axis=0).astype(jnp.float32)
        spectra = jnp.dot(picked, forward_wide, preferred_element_type=jnp.float32) * factor
        far_all.append(spectra.astype(jnp.bfloat16))

    def one_block(shot_block):
        summed = jnp.zeros((shot_block.shape[0], receivers, 2 * F), jnp.float32)
        for group_index in range(N_SURF):
            points = surface_point[:, group_index, :].reshape(-1)
            columns = jnp.take(shot_block, points, axis=1).astype(jnp.float32)
            near_spec = (jnp.dot(columns, forward_wide, preferred_element_type=jnp.float32) * factor).astype(jnp.bfloat16)
            partial_value = spectral_product(near_spec, far_all[group_index], F).astype(jnp.bfloat16)
            partial_value = lax.optimization_barrier(partial_value)
            summed = summed + partial_value.astype(jnp.float32)
        spectrum = summed.astype(jnp.bfloat16).astype(jnp.float32)
        result = lax.dot_general(spectrum, forward_wide, (((2,), (1,)), ((), ())), preferred_element_type=jnp.float32)
        return (result * (-factor)).astype(jnp.bfloat16)

    blocks = traces.reshape(shot_total // SHOT_DEV, SHOT_DEV, receivers, samples)
    return lax.map(one_block, blocks).reshape(shot_total, receivers, samples)
```

```python
import math

import jax
import jax.numpy as jnp
from jax import lax
from jax.sharding import PartitionSpec as P

F = 256


def dft_rows(samples, owners):
    bins = F // owners
    freq = jnp.arange(F, dtype=jnp.int32).reshape(owners, 1, bins, 1)
    time = jnp.arange(samples, dtype=jnp.int32)
    angles = (freq * time % samples).astype(jnp.float32) * (2.0 * math.pi / samples)
    table = jnp.concatenate([jnp.cos(angles), -jnp.sin(angles)], axis=1)
    return table.astype(jnp.bfloat16).reshape(2 * F, samples)


def shards(traces, surface_point, gather_index):
    shots, receivers, samples = traces.shape
    owners = lax.axis_size("shot")
    share = receivers // lax.axis_size("surf")
    bins = F // owners
    forward = dft_rows(samples, owners)
    factor = samples**-0.5
    points = surface_point.reshape(-1)
    sources = gather_index.reshape(-1)
    count = points.shape[0]
    block = lax.dynamic_slice_in_dim(traces, lax.axis_index("surf") * share, share, axis=1)
    rows = jnp.concatenate([block, jnp.take(traces, points, axis=1)], axis=1)
    spectra = lax.dot_general(
        forward, rows, (((1,), (2,)), ((), ())), preferred_element_type=jnp.float32
    )
    spectra = (spectra * factor).astype(jnp.bfloat16)
    spectra = spectra.reshape(owners, 2 * bins, shots, share + count)
    here = lax.all_to_all(spectra, "shot", 0, 0, tiled=True)
    here = here.reshape(owners, 2, bins, shots, share + count)
    far = here[sources // shots, :, :, sources % shots, :share]
    near = here[..., share:].transpose(2, 0, 3, 1, 4).reshape(bins, owners * shots, 2 * count)
    far = far.transpose(2, 1, 0, 3)
    right = jnp.concatenate(
        [
            jnp.concatenate([far[:, 0], far[:, 1]], axis=2),
            jnp.concatenate([-far[:, 1], far[:, 0]], axis=2),
        ],
        axis=1,
    )
    total = jnp.einsum("bsk,bkr->bsr", near, right, preferred_element_type=jnp.float32)
    total = total.astype(jnp.bfloat16).reshape(bins, owners, shots, 2, share)
    total = total.transpose(1, 3, 0, 2, 4).reshape(owners, 2 * bins, shots, share)
    back = lax.all_to_all(total, "shot", 0, 0, tiled=True)
    back = back.reshape(2 * F, shots, share)
    result = lax.dot_general(
        back, forward, (((0,), (0,)), ((), ())), preferred_element_type=jnp.float32
    )
    return (result * -factor).astype(jnp.bfloat16)


def solution(mesh):
    placed = (P("shot", None, None), P(), P())
    return jax.shard_map(
        shards, mesh=mesh, in_specs=placed, out_specs=P("shot", "surf", None), check_vma=False
    )
```

```python
import functools
import math

import jax
import jax.numpy as jnp
import ml_dtypes
import numpy as np
from jax import lax
from jax.experimental import pallas as pl
from jax.experimental.pallas import tpu as pltpu
from jax.sharding import PartitionSpec as P

F = 256
OWNERS = 32
BINS = F // OWNERS
PART = 2 * BINS
SHOTS = 8
POINTS = 32
MAIN, TAIL = 128, 32
SHARE = MAIN + TAIL
WIDE = SHOTS * TAIL
MESH = pl.DeviceIdType.MESH
F32, BF16 = jnp.float32, jnp.bfloat16


def dft_rows(samples):
    freq = np.arange(F).reshape(OWNERS, 1, BINS, 1)
    angles = (freq * np.arange(samples) % samples) * (2.0 * math.pi / samples)
    table = np.concatenate([np.cos(angles), -np.sin(angles)], axis=1)
    table = table.astype(np.float32).astype(ml_dtypes.bfloat16).astype(np.float32)
    scaled = table.reshape(2 * F, samples) * samples**-0.5
    return scaled.astype(ml_dtypes.bfloat16)


def offsets():
    steps = [(z, x, y) for z in range(2) for x in range(4) for y in range(4)][1:]
    return sorted(steps, key=lambda k: -(k[0] + min(k[1], 4 - k[1]) + min(k[2], 4 - k[2])))


def halves(array):
    return array[:, :MAIN], array[:, MAIN:]


def wide_rows(ref, rows):
    return jnp.concatenate([ref[half, rows, :] for half in range(2)], axis=1)


def dot(a, b, contract):
    return lax.dot_general(a, b, (contract, ((), ())), preferred_element_type=F32)


def kernel(
    points, gathers, traces, table, out,
    tab, xm, xt, full, xn, sm, sn, st, rm, rn, rt,
    near, far_main, far_tail, om, ot, bm, bt, hm, ht, ov,
    load_sem, own_sem, send_sem, recv_sem,
):
    group, me = lax.axis_index("surf"), lax.axis_index("shot")
    z, x, y = me // 16, (me // 4) % 4, me % 4
    peers = [(z ^ k) * 16 + (x + i) % 4 * 4 + (y + j) % 4 for k, i, j in offsets()]
    first = group * SHARE

    loads = [
        pltpu.make_async_copy(table, tab, load_sem.at[0]),
        pltpu.make_async_copy(traces.at[:, pl.ds(first, MAIN), :], xm, load_sem.at[1]),
        pltpu.make_async_copy(traces.at[:, pl.ds(first + MAIN, TAIL), :], xt, load_sem.at[2]),
        pltpu.make_async_copy(traces, full, load_sem.at[3]),
    ]
    for load in loads:
        load.start()
    barrier = pltpu.get_barrier_semaphore()
    for peer in peers:
        pl.semaphore_signal(barrier, inc=1, device_id=(group, peer), device_id_type=MESH)

    def exchange(kind, source, target):
        own = pltpu.make_async_copy(source.at[me], target(me), own_sem.at[kind])
        own.start()
        copies = [own]
        for k, peer in enumerate(peers):
            copy = pltpu.make_async_remote_copy(
                src_ref=source.at[peer],
                dst_ref=target(me),
                send_sem=send_sem.at[kind, k],
                recv_sem=recv_sem.at[kind, k],
                device_id=(group, peer),
                device_id_type=MESH,
            )
            copy.start()
            copies.append(copy)
        return copies

    def arrive(copies):
        copies[0].wait()
        for copy in copies[1:]:
            copy.wait_recv()

    def forward(rows):
        spectra = dot(tab[...], rows, ((1,), (1,))).astype(BF16)
        return spectra.reshape(OWNERS, PART, WIDE)

    loads[0].wait()
    loads[1].wait()
    for k in range(SHOTS // 2):
        spectra = forward(xm[2 * k : 2 * k + 2].reshape(WIDE, -1))
        for half, value in enumerate((spectra[..., :MAIN], spectra[..., MAIN:])):
            sm[:, 2 * k + half] = value
    pl.semaphore_wait(barrier, len(peers))
    mains = exchange(0, sm, lambda device: rm.at[pl.ds(device * SHOTS, SHOTS)])

    chosen = jnp.zeros((POINTS, 1), jnp.int32)
    position = lax.broadcasted_iota(jnp.int32, (POINTS, 1), 0)
    for i in range(POINTS):
        chosen = jnp.where(position == i, points[i], chosen)
    receivers = full.shape[1]
    pick = (lax.broadcasted_iota(jnp.int32, (POINTS, receivers), 1) == chosen).astype(BF16)
    loads[3].wait()
    for s in range(SHOTS):
        xn[s * POINTS : (s + 1) * POINTS, :] = dot(pick, full[s], ((1,), (0,))).astype(BF16)
    sn[...] = forward(xn[...])
    nears = exchange(1, sn, lambda device: rn.at[device])
    loads[2].wait()
    st[...] = forward(xt[...].reshape(WIDE, -1))
    tails = exchange(2, st, lambda device: rt.at[device])

    block = lambda axis: lax.broadcasted_iota(jnp.int32, (WIDE, WIDE), axis) // TAIL
    diagonal = (block(0) == block(1)).astype(BF16)
    tile = lambda a: jnp.concatenate([a] * SHOTS, axis=0)
    arrive(mains)
    for i in range(POINTS):
        far_main[i * PART : (i + 1) * PART, :] = rm[gathers[i]].astype(F32)
    arrive(nears)
    for half, value in enumerate(halves(rn[...].reshape(OWNERS * PART, WIDE))):
        near[half] = value.astype(F32)
    for b in range(BINS):
        rows = [pl.ds(b, OWNERS, stride=PART), pl.ds(BINS + b, OWNERS, stride=PART)]
        left = [tile(wide_rows(near, r).astype(BF16)) * diagonal for r in rows]
        real, imag = [tile(far_main[r, :].astype(BF16)) for r in rows]
        right = jnp.concatenate(
            [jnp.concatenate([real, imag], axis=1), jnp.concatenate([-imag, real], axis=1)], axis=0
        )
        total = -dot(jnp.concatenate(left, axis=1), right, ((1,), (0,)))
        for s in range(SHOTS):
            for part in range(2):
                om[pl.ds(s * PART + part * BINS + b, OWNERS, stride=SHOTS * PART), :] = total[
                    s * OWNERS : (s + 1) * OWNERS, part * MAIN : (part + 1) * MAIN
                ]
    totals = om[...].reshape(OWNERS, SHOTS, PART, MAIN)
    for s in range(SHOTS):
        bm[:, :, s * MAIN : (s + 1) * MAIN] = totals[:, s].astype(BF16)
    back_mains = exchange(3, bm, lambda device: hm.at[device])

    arrive(tails)
    fold = lambda axis: lax.broadcasted_iota(jnp.int32, (WIDE, WIDE), axis) % TAIL
    spread = (fold(0) == fold(1)).astype(BF16)
    shot_of = lax.broadcasted_iota(jnp.int32, (PART, WIDE), 1) // TAIL
    picked = []
    for i in range(POINTS):
        owner, local = lax.div(gathers[i], SHOTS), lax.rem(gathers[i], SHOTS)
        picked.append(rt[owner] * (shot_of == local).astype(BF16))
    for half, value in enumerate(halves(dot(jnp.concatenate(picked, axis=0), spread, ((1,), (0,))))):
        far_tail[half] = value
    for b in range(BINS):
        rows = [pl.ds(b, OWNERS, stride=PART), pl.ds(BINS + b, OWNERS, stride=PART)]
        left = jnp.concatenate([wide_rows(near, r).astype(BF16) for r in rows], axis=1)
        real, imag = [tile(wide_rows(far_tail, r).astype(BF16)) * diagonal for r in rows]
        right = jnp.concatenate(
            [jnp.concatenate([real, imag], axis=1), jnp.concatenate([-imag, real], axis=1)], axis=0
        )
        total = -dot(left, right, ((1,), (0,)))
        for part in range(2):
            for half in range(2):
                lanes = slice(part * WIDE + half * MAIN, part * WIDE + (half + 1) * MAIN)
                ot[half, rows[part], :] = total[:, lanes]
    for half in range(2):
        lanes = slice(half * MAIN, (half + 1) * MAIN)
        bt[:, :, lanes] = ot[half].reshape(OWNERS, PART, MAIN).astype(BF16)
    back_tails = exchange(4, bt, lambda device: ht.at[device])

    arrive(back_mains)
    for k in range(SHOTS // 2):
        spectrum = hm[:, :, k * WIDE : (k + 1) * WIDE].reshape(2 * F, WIDE)
        series = dot(spectrum, tab[...], ((0,), (0,))).astype(BF16)
        ov[2 * k : 2 * k + 2, :MAIN, :] = series.reshape(2, MAIN, -1)
    arrive(back_tails)
    series = dot(ht[...].reshape(2 * F, WIDE), tab[...], ((0,), (0,))).astype(BF16)
    ov[:, MAIN:, :] = series.reshape(SHOTS, TAIL, -1)
    store = pltpu.make_async_copy(ov, out, load_sem.at[0])
    store.start()
    for copies in (mains, nears, tails, back_mains, back_tails):
        for copy in copies[1:]:
            copy.wait_send()
    store.wait()


def shards(traces, surface_point, gather_index):
    shots, receivers, samples = traces.shape
    vmem = lambda *shape, dtype=BF16: pltpu.VMEM(shape, dtype)
    smem, hbm = pl.BlockSpec(memory_space=pltpu.SMEM), pl.BlockSpec(memory_space=pl.ANY)
    message = lambda lanes: vmem(OWNERS, PART, lanes)
    return pl.pallas_call(
        kernel,
        out_shape=jax.ShapeDtypeStruct((shots, SHARE, samples), BF16),
        in_specs=[smem, smem, hbm, hbm],
        out_specs=hbm,
        scratch_shapes=[
            vmem(2 * F, samples),
            vmem(SHOTS, MAIN, samples),
            vmem(SHOTS, TAIL, samples),
            vmem(SHOTS, receivers, samples),
            vmem(WIDE, samples),
            vmem(OWNERS, SHOTS, PART, MAIN),
            message(WIDE),
            message(WIDE),
            vmem(OWNERS * SHOTS, PART, MAIN),
            message(WIDE),
            message(WIDE),
            vmem(2, OWNERS * PART, MAIN, dtype=F32),
            vmem(POINTS * PART, MAIN, dtype=F32),
            vmem(2, POINTS * PART, MAIN, dtype=F32),
            vmem(OWNERS * SHOTS * PART, MAIN, dtype=F32),
            vmem(2, OWNERS * PART, MAIN, dtype=F32),
            *[message(lanes) for lanes in (SHOTS * MAIN, WIDE) * 2],
            vmem(SHOTS, SHARE, samples),
            pltpu.SemaphoreType.DMA((4,)),
            pltpu.SemaphoreType.DMA((5,)),
            pltpu.SemaphoreType.DMA((5, OWNERS - 1)),
            pltpu.SemaphoreType.DMA((5, OWNERS - 1)),
        ],
        compiler_params=pltpu.CompilerParams(
            collective_id=0, has_side_effects=True, vmem_limit_bytes=56 * 2**20
        ),
    )(surface_point.reshape(-1), gather_index.reshape(-1), traces, jnp.asarray(dft_rows(samples)))


def solution(mesh):
    placed = (P("shot", None, None), P(), P())
    return jax.shard_map(
        shards, mesh=mesh, in_specs=placed, out_specs=P("shot", "surf", None), check_vma=False
    )
```

```python
import functools
import math

import jax
import jax.numpy as jnp
import ml_dtypes
import numpy as np
from jax import lax
from jax.experimental import pallas as pl
from jax.experimental.pallas import tpu as pltpu
from jax.sharding import PartitionSpec as P

F = 256
OWNERS = 32
BINS = F // OWNERS
PART = 2 * BINS
SHOTS = 8
POINTS = 32
MAIN, TAIL = 128, 32
SHARE = MAIN + TAIL
HALF = POINTS // 2
WIDE = SHOTS * TAIL
MESH = pl.DeviceIdType.MESH
F32, BF16 = jnp.float32, jnp.bfloat16


def dft_rows(samples):
    freq = np.arange(F).reshape(OWNERS, 1, BINS, 1)
    angles = (freq * np.arange(samples) % samples) * (2.0 * math.pi / samples)
    table = np.concatenate([np.cos(angles), -np.sin(angles)], axis=1)
    table = table.astype(np.float32).astype(ml_dtypes.bfloat16).astype(np.float32)
    scaled = table.reshape(2 * F, samples) * samples**-0.5
    return scaled.astype(ml_dtypes.bfloat16)


def offsets():
    steps = [(z, x, y) for z in range(2) for x in range(4) for y in range(4)][1:]
    return sorted(steps, key=lambda k: -(k[0] + min(k[1], 4 - k[1]) + min(k[2], 4 - k[2])))


def wide_rows(ref, rows):
    return jnp.concatenate([ref[half, rows, :] for half in range(2)], axis=1)


def dot(a, b, contract):
    return lax.dot_general(a, b, (contract, ((), ())), preferred_element_type=F32)


def iota(shape, axis):
    return lax.broadcasted_iota(jnp.int32, shape, axis)


def product(left, right):
    real, imag = right
    both = jnp.concatenate(
        [jnp.concatenate([real, imag], axis=1), jnp.concatenate([-imag, real], axis=1)], axis=0
    )
    return dot(left, both, ((1,), (0,)))


def kernel(
    point_ref, gather_ref, traces, table, hm, ht,
    points, gathers, tab, full, xn, sm, sn, st, rm, rn, other, rt,
    near, lhs, far_main, far_tail, om, ot, bm, bt,
    load_sem, pair_sem, ready, send_sem, recv_sem,
):
    group, me = lax.axis_index("surf"), lax.axis_index("shot")
    core = group % 2
    z, x, y = me // 16, (me // 4) % 4, me % 4
    peers = [(z ^ k) * 16 + (x + i) % 4 * 4 + (y + j) % 4 for k, i, j in offsets()]
    away = lambda d: [n for n, step in enumerate(offsets()) if sum(map(bool, step)) == d]
    groups = lax.axis_size("surf")

    share = SHARE // PART
    blocks = [pl.ds((group + k) % groups * share, share) for k in range(groups)]
    loads = [pltpu.make_async_copy(table, tab, load_sem.at[0])]
    for k, block in enumerate(blocks):
        loads.append(pltpu.make_async_copy(traces.at[:, block], full.at[:, block], load_sem.at[1 + k]))
    loads.append(pltpu.make_async_copy(point_ref, points, load_sem.at[5]))
    loads.append(pltpu.make_async_copy(gather_ref, gathers, load_sem.at[6]))
    for load in loads:
        load.start()
    barrier = pltpu.get_barrier_semaphore()
    greetings = [barrier, ready.at[0], ready.at[1]]

    def greet(stage):
        for n in away(1):
            pl.semaphore_signal(
                greetings[stage], inc=1, device_id=(group, peers[n]), device_id_type=MESH
            )

    pl.semaphore_signal(barrier, inc=1, device_id=(group ^ 1, me), device_id_type=MESH)
    greet(0)

    def start(way, which):
        kind, source, target = way
        for n in which:
            pltpu.make_async_remote_copy(
                src_ref=source(peers[n]),
                dst_ref=target(me),
                send_sem=send_sem.at[kind],
                recv_sem=recv_sem.at[kind],
                device_id=(group, peers[n]),
                device_id_type=MESH,
            ).start()

    def keep(way):
        kind, source, target = way
        pltpu.make_async_copy(source(me), target(me), recv_sem.at[kind]).start()

    def arrive(kind, whole):
        pltpu.make_async_copy(whole, whole, recv_sem.at[kind]).wait()

    def sent(kind, whole):
        others = whole.at[pl.ds(0, OWNERS - 1)]
        pltpu.make_async_copy(others, others, send_sem.at[kind]).wait()

    def forward(rows):
        spectra = dot(tab[...], rows, ((1,), (1,))).astype(BF16)
        return spectra.reshape(OWNERS, PART, -1)

    slot = lambda ref: lambda device: ref.at[device]
    two = lambda ref, k: lambda device: ref.at[device, pl.ds(2 * k, 2)]
    pairs = range(SHOTS // 2)
    everyone = away(3) + away(2) + away(1)
    tail_way, near_way = (0, slot(st), slot(rt)), (1, slot(sn), slot(rn))
    main_ways = [(2, two(sm, k), two(rm, k)) for k in pairs]

    loads[0].wait()
    loads[1].wait()
    own = group * share
    main = pl.ds(own, MAIN // PART)
    tail = pl.ds(own + MAIN // PART, TAIL // PART)
    st[...] = forward(full[:, tail].reshape(WIDE, -1))
    for k in pairs:
        spectra = forward(full[2 * k : 2 * k + 2, main].reshape(2 * MAIN, -1))
        sm[:, 2 * k] = spectra[..., :MAIN]
        sm[:, 2 * k + 1] = spectra[..., MAIN:]
    for way in (tail_way, *main_ways):
        keep(way)
    pl.semaphore_wait(barrier, len(away(1)) + 1)
    greet(1)
    for way in (tail_way, *main_ways):
        start(way, away(1))

    for load in loads[2:]:
        load.wait()
    chosen = jnp.zeros((HALF, 1), jnp.int32)
    aligned = []
    for i in range(HALF):
        point = points[core * 2 + i // 8, i // 4 % 2, i % 4]
        aligned.append(lax.div(point, PART))
        chosen = jnp.where(iota((HALF, 1), 0) == i, i * PART + lax.rem(point, PART), chosen)
    pick = (iota((HALF, HALF * PART), 1) == chosen).astype(BF16)
    for s in range(SHOTS):
        rows = jnp.concatenate([full[s, row] for row in aligned], axis=0)
        xn[s * HALF : (s + 1) * HALF, :] = dot(pick, rows, ((1,), (0,))).astype(BF16)
    sn[...] = forward(xn[...])
    keep(near_way)
    start(near_way, away(1))
    pl.semaphore_wait(greetings[1], len(away(1)))
    greet(2)
    for way in (tail_way, near_way, *main_ways[:2]):
        start(way, away(2))
    pl.semaphore_wait(greetings[2], len(away(1)))
    for way in (tail_way, near_way):
        start(way, away(3))
    for way in main_ways[:2]:
        start(way, away(3))
    for way in main_ways[2:]:
        start(way, away(3) + away(2))

    lines = [[pl.ds(part * BINS + b, OWNERS, stride=PART) for part in range(2)] for b in range(BINS)]
    local_of = iota((PART, WIDE), 1) // TAIL
    spread = (iota((WIDE, WIDE), 0) % TAIL == iota((WIDE, WIDE), 1) % TAIL).astype(BF16)
    shot_of_point = lambda axis: iota((WIDE, WIDE), axis) % MAIN // HALF
    tile = lambda a: jnp.concatenate([a[:HALF]] * SHOTS + [a[HALF:]] * SHOTS, axis=0)
    index = lambda i: gathers[i // 8, i // 4 % 2, i % 4]

    arrive(0, rt)
    picked = []
    for i in range(POINTS):
        mask = (local_of == lax.rem(index(i), SHOTS)).astype(BF16)
        picked.append(rt[lax.div(index(i), SHOTS)] * mask)
    spectra = dot(jnp.concatenate(picked, axis=0), spread, ((1,), (0,)))
    for half in range(2):
        far_tail[half] = spectra[:, half * MAIN : (half + 1) * MAIN]
    arrive(1, rn)
    swap = pltpu.make_async_remote_copy(
        src_ref=rn,
        dst_ref=other,
        send_sem=pair_sem.at[0],
        recv_sem=pair_sem.at[1],
        device_id=(group ^ 1, me),
        device_id_type=MESH,
    )
    swap.start()
    near[core] = rn[...].reshape(OWNERS * PART, MAIN).astype(F32)
    swap.wait()
    near[1 - core] = other[...].reshape(OWNERS * PART, MAIN).astype(F32)
    diagonal = (shot_of_point(0) == iota((WIDE, WIDE), 1) // TAIL).astype(BF16)
    for b in range(BINS):
        left = jnp.concatenate([wide_rows(near, r).astype(BF16) for r in lines[b]], axis=1)
        right = [tile(wide_rows(far_tail, r).astype(BF16)) * diagonal for r in lines[b]]
        total = -product(left, right)
        for part in range(2):
            for half in range(2):
                lanes = slice(part * WIDE + half * MAIN, part * WIDE + (half + 1) * MAIN)
                ot[half, lines[b][part], :] = total[:, lanes]
    for half in range(2):
        lanes = slice(half * MAIN, (half + 1) * MAIN)
        bt[:, :, lanes] = ot[half].reshape(OWNERS, PART, MAIN).astype(BF16)
    back_tail = 3, slot(bt), slot(ht)
    keep(back_tail)
    start(back_tail, everyone)
    diagonal = (iota((WIDE, WIDE), 0) // OWNERS == shot_of_point(1)).astype(BF16)
    for b in range(BINS):
        for part, r in enumerate(lines[b]):
            copies = [wide_rows(near, r).astype(BF16)] * SHOTS
            lhs[b, :, part * WIDE : (part + 1) * WIDE] = jnp.concatenate(copies, axis=0) * diagonal

    arrive(2, rm)
    for i in range(POINTS):
        far = rm[lax.div(index(i), SHOTS), lax.rem(index(i), SHOTS)]
        far_main[i * PART : (i + 1) * PART, :] = far.astype(F32)
    for b in range(BINS):
        total = -product(lhs[b], [tile(far_main[r, :].astype(BF16)) for r in lines[b]])
        for s in range(SHOTS):
            for part in range(2):
                om[pl.ds(s * PART + part * BINS + b, OWNERS, stride=SHOTS * PART), :] = total[
                    s * OWNERS : (s + 1) * OWNERS, part * MAIN : (part + 1) * MAIN
                ]
    totals = om[...].reshape(OWNERS, SHOTS, PART, MAIN)
    for k in pairs:
        bm[:, 2 * k : 2 * k + 2] = totals[:, 2 * k : 2 * k + 2].astype(BF16)
        back_main = 4, two(bm, k), two(hm, k)
        keep(back_main)
        start(back_main, everyone)
    arrive(3, ht)
    arrive(4, hm)
    for kind, whole in enumerate((st, sn, sm, bt, bm)):
        sent(kind, whole)


def inverse(hm, ht, table, out, hm_v, ht_v, tab, series, load_sem, store_sem):
    shots = out.shape[0]
    pairs = range(shots // 2)
    loads = [
        pltpu.make_async_copy(table, tab, load_sem.at[0]),
        pltpu.make_async_copy(ht, ht_v, load_sem.at[1]),
        *[
            pltpu.make_async_copy(hm.at[:, pl.ds(2 * k, 2)], hm_v.at[k], load_sem.at[2 + k])
            for k in pairs
        ],
    ]
    for load in loads:
        load.start()
    invert = lambda spectra: dot(spectra, tab[...], ((0,), (0,))).astype(BF16)
    loads[0].wait()
    loads[1].wait()
    series[:, MAIN:, :] = invert(ht_v[...].reshape(2 * F, WIDE)).reshape(shots, TAIL, -1)
    stores = []
    for k in pairs:
        loads[2 + k].wait()
        two = pl.ds(2 * k, 2)
        spectra = [hm_v[k, :, s].reshape(2 * F, MAIN) for s in range(2)]
        series[two, :MAIN, :] = invert(jnp.concatenate(spectra, axis=1)).reshape(2, MAIN, -1)
        stores.append(pltpu.make_async_copy(series.at[two], out.at[two], store_sem.at[k]))
        stores[-1].start()
    for store in stores:
        store.wait()


def shards(traces, surface_point, gather_index):
    shots, receivers, samples = traces.shape
    vmem = lambda *shape, dtype=BF16: pltpu.VMEM(shape, dtype)
    hbm, anywhere = pl.BlockSpec(memory_space=pltpu.HBM), pl.BlockSpec(memory_space=pl.ANY)
    message = lambda lanes: vmem(OWNERS, PART, lanes)
    table = jnp.asarray(dft_rows(samples))
    back = [
        jax.ShapeDtypeStruct((OWNERS, SHOTS, PART, MAIN), BF16),
        jax.ShapeDtypeStruct((OWNERS, PART, WIDE), BF16),
    ]
    spectra = pl.pallas_call(
        kernel,
        out_shape=back,
        in_specs=[hbm] * 4,
        out_specs=[anywhere, anywhere],
        scratch_shapes=[
            pltpu.SMEM((4, 2, 4), jnp.int32),
            pltpu.SMEM((4, 2, 4), jnp.int32),
            vmem(2 * F, samples),
            vmem(SHOTS, receivers // PART, PART, samples),
            vmem(SHOTS * HALF, samples),
            vmem(OWNERS, SHOTS, PART, MAIN),
            message(MAIN),
            message(WIDE),
            vmem(OWNERS, SHOTS, PART, MAIN),
            message(MAIN),
            message(MAIN),
            message(WIDE),
            vmem(2, OWNERS * PART, MAIN, dtype=F32),
            vmem(BINS, WIDE, 2 * WIDE),
            vmem(POINTS * PART, MAIN, dtype=F32),
            vmem(2, POINTS * PART, MAIN, dtype=F32),
            vmem(OWNERS * SHOTS * PART, MAIN, dtype=F32),
            vmem(2, OWNERS * PART, MAIN, dtype=F32),
            vmem(OWNERS, SHOTS, PART, MAIN),
            message(WIDE),
            pltpu.SemaphoreType.DMA((7,)),
            pltpu.SemaphoreType.DMA((2,)),
            pltpu.SemaphoreType.REGULAR((2,)),
            pltpu.SemaphoreType.DMA((5,)),
            pltpu.SemaphoreType.DMA((5,)),
        ],
        compiler_params=pltpu.CompilerParams(
            collective_id=0, has_side_effects=True, vmem_limit_bytes=61 * 2**20
        ),
    )(
        surface_point.transpose(0, 2, 1),
        gather_index.transpose(0, 2, 1),
        traces.reshape(shots, receivers // PART, PART, samples),
        table,
    )
    return pl.pallas_call(
        inverse,
        out_shape=jax.ShapeDtypeStruct((shots, SHARE, samples), BF16),
        in_specs=[anywhere] * 3,
        out_specs=anywhere,
        scratch_shapes=[
            vmem(SHOTS // 2, OWNERS, 2, PART, MAIN),
            message(WIDE),
            vmem(2 * F, samples),
            vmem(SHOTS, SHARE, samples),
            pltpu.SemaphoreType.DMA((2 + SHOTS // 2,)),
            pltpu.SemaphoreType.DMA((SHOTS // 2,)),
        ],
        compiler_params=pltpu.CompilerParams(vmem_limit_bytes=61 * 2**20),
    )(*spectra, table)


def solution(mesh):
    placed = (P("shot", None, None), P(), P())
    return jax.shard_map(
        shards, mesh=mesh, in_specs=placed, out_specs=P("shot", "surf", None), check_vma=False
    )
```

```python
import functools
import math

import jax
import jax.numpy as jnp
import ml_dtypes
import numpy as np
from jax import lax
from jax.experimental import pallas as pl
from jax.experimental.pallas import tpu as pltpu
from jax.sharding import PartitionSpec as P

F = 256
OWNERS = 32
BINS = F // OWNERS
PART = 2 * BINS
SHOTS = 8
POINTS = 32
MAIN, TAIL = 128, 32
SHARE = MAIN + TAIL
HALF = POINTS // 2
WIDE = SHOTS * TAIL
MESH = pl.DeviceIdType.MESH
F32, BF16 = jnp.float32, jnp.bfloat16


def dft_rows(samples):
    freq = np.arange(F).reshape(OWNERS, 1, BINS, 1)
    angles = (freq * np.arange(samples) % samples) * (2.0 * math.pi / samples)
    table = np.concatenate([np.cos(angles), -np.sin(angles)], axis=1)
    table = table.astype(np.float32).astype(ml_dtypes.bfloat16).astype(np.float32)
    scaled = table.reshape(2 * F, samples) * samples**-0.5
    return scaled.astype(ml_dtypes.bfloat16)


def offsets():
    steps = [(z, x, y) for z in range(2) for x in range(4) for y in range(4)][1:]
    return sorted(steps, key=lambda k: -(k[0] + min(k[1], 4 - k[1]) + min(k[2], 4 - k[2])))


def wide_rows(ref, rows):
    return jnp.concatenate([ref[half, rows, :] for half in range(2)], axis=1)


def dot(a, b, contract):
    return lax.dot_general(a, b, (contract, ((), ())), preferred_element_type=F32)


def iota(shape, axis):
    return lax.broadcasted_iota(jnp.int32, shape, axis)


def product(left, right):
    real, imag = right
    both = jnp.concatenate(
        [jnp.concatenate([real, imag], axis=1), jnp.concatenate([-imag, real], axis=1)], axis=0
    )
    return dot(left, both, ((1,), (0,)))


def kernel(
    point_ref, gather_ref, traces, table, hm, ht,
    points, gathers, tab, full, xn, sm, sn, st, rm, rn, other, rt,
    near, lhs, far_main, far_tail, om, ot, bm, bt,
    load_sem, pair_sem, ready, send_sem, recv_sem,
):
    group, me = lax.axis_index("surf"), lax.axis_index("shot")
    core = group % 2
    z, x, y = me // 16, (me // 4) % 4, me % 4
    peers = [(z ^ k) * 16 + (x + i) % 4 * 4 + (y + j) % 4 for k, i, j in offsets()]
    away = lambda d: [n for n, step in enumerate(offsets()) if sum(map(bool, step)) == d]
    groups = lax.axis_size("surf")

    share = SHARE // PART
    blocks = [pl.ds((group + k) % groups * share, share) for k in range(groups)]
    loads = [pltpu.make_async_copy(table, tab, load_sem.at[0])]
    for k, block in enumerate(blocks):
        loads.append(pltpu.make_async_copy(traces.at[:, block], full.at[:, block], load_sem.at[1 + k]))
    loads.append(pltpu.make_async_copy(point_ref, points, load_sem.at[5]))
    loads.append(pltpu.make_async_copy(gather_ref, gathers, load_sem.at[6]))
    for load in loads:
        load.start()
    barrier = pltpu.get_barrier_semaphore()
    greetings = [barrier, ready.at[0], ready.at[1]]

    def greet(stage):
        for n in away(1) + away(2) + away(3) if stage == 0 else []:
            pl.semaphore_signal(
                greetings[stage], inc=1, device_id=(group, peers[n]), device_id_type=MESH
            )

    pl.semaphore_signal(barrier, inc=1, device_id=(group ^ 1, me), device_id_type=MESH)
    greet(0)

    def start(way, which):
        kind, source, target = way
        for n in which:
            pltpu.make_async_remote_copy(
                src_ref=source(peers[n]),
                dst_ref=target(me),
                send_sem=send_sem.at[kind],
                recv_sem=recv_sem.at[kind],
                device_id=(group, peers[n]),
                device_id_type=MESH,
            ).start()

    def keep(way):
        kind, source, target = way
        pltpu.make_async_copy(source(me), target(me), recv_sem.at[kind]).start()

    def arrive(kind, whole):
        pltpu.make_async_copy(whole, whole, recv_sem.at[kind]).wait()

    def sent(kind, whole):
        others = whole.at[pl.ds(0, OWNERS - 1)]
        pltpu.make_async_copy(others, others, send_sem.at[kind]).wait()

    def forward(rows):
        spectra = dot(tab[...], rows, ((1,), (1,))).astype(BF16)
        return spectra.reshape(OWNERS, PART, -1)

    slot = lambda ref: lambda device: ref.at[device]
    two = lambda ref, k: lambda device: ref.at[device, pl.ds(2 * k, 2)]
    pairs = range(SHOTS // 2)
    everyone = away(3) + away(2) + away(1)
    tail_way, near_way = (0, slot(st), slot(rt)), (1, slot(sn), slot(rn))
    main_ways = [(2, two(sm, k), two(rm, k)) for k in pairs]

    loads[0].wait()
    loads[1].wait()
    own = group * share
    main = pl.ds(own, MAIN // PART)
    tail = pl.ds(own + MAIN // PART, TAIL // PART)
    st[...] = forward(full[:, tail].reshape(WIDE, -1))
    for k in pairs:
        spectra = forward(full[2 * k : 2 * k + 2, main].reshape(2 * MAIN, -1))
        sm[:, 2 * k] = spectra[..., :MAIN]
        sm[:, 2 * k + 1] = spectra[..., MAIN:]
    for way in (tail_way, *main_ways):
        keep(way)
    pl.semaphore_wait(barrier, 32)
    greet(1)
    for way in (tail_way, *main_ways[:2]):
        start(way, everyone)

    for load in loads[2:]:
        load.wait()
    chosen = jnp.zeros((HALF, 1), jnp.int32)
    aligned = []
    for i in range(HALF):
        point = points[core * 2 + i // 8, i // 4 % 2, i % 4]
        aligned.append(lax.div(point, PART))
        chosen = jnp.where(iota((HALF, 1), 0) == i, i * PART + lax.rem(point, PART), chosen)
    pick = (iota((HALF, HALF * PART), 1) == chosen).astype(BF16)
    for s in range(SHOTS):
        rows = jnp.concatenate([full[s, row] for row in aligned], axis=0)
        xn[s * HALF : (s + 1) * HALF, :] = dot(pick, rows, ((1,), (0,))).astype(BF16)
    sn[...] = forward(xn[...])
    keep(near_way)
    start(near_way, everyone)
    for way in main_ways[2:]:
        start(way, everyone)

    lines = [[pl.ds(part * BINS + b, OWNERS, stride=PART) for part in range(2)] for b in range(BINS)]
    local_of = iota((PART, WIDE), 1) // TAIL
    spread = (iota((WIDE, WIDE), 0) % TAIL == iota((WIDE, WIDE), 1) % TAIL).astype(BF16)
    shot_of_point = lambda axis: iota((WIDE, WIDE), axis) % MAIN // HALF
    tile = lambda a: jnp.concatenate([a[:HALF]] * SHOTS + [a[HALF:]] * SHOTS, axis=0)
    index = lambda i: gathers[i // 8, i // 4 % 2, i % 4]

    arrive(0, rt)
    picked = []
    for i in range(POINTS):
        mask = (local_of == lax.rem(index(i), SHOTS)).astype(BF16)
        picked.append(rt[lax.div(index(i), SHOTS)] * mask)
    spectra = dot(jnp.concatenate(picked, axis=0), spread, ((1,), (0,)))
    for half in range(2):
        far_tail[half] = spectra[:, half * MAIN : (half + 1) * MAIN]
    arrive(1, rn)
    swap = pltpu.make_async_remote_copy(
        src_ref=rn,
        dst_ref=other,
        send_sem=pair_sem.at[0],
        recv_sem=pair_sem.at[1],
        device_id=(group ^ 1, me),
        device_id_type=MESH,
    )
    swap.start()
    near[core] = rn[...].reshape(OWNERS * PART, MAIN).astype(F32)
    swap.wait()
    near[1 - core] = other[...].reshape(OWNERS * PART, MAIN).astype(F32)
    diagonal = (shot_of_point(0) == iota((WIDE, WIDE), 1) // TAIL).astype(BF16)
    for b in range(BINS):
        left = jnp.concatenate([wide_rows(near, r).astype(BF16) for r in lines[b]], axis=1)
        right = [tile(wide_rows(far_tail, r).astype(BF16)) * diagonal for r in lines[b]]
        total = -product(left, right)
        for part in range(2):
            for half in range(2):
                lanes = slice(part * WIDE + half * MAIN, part * WIDE + (half + 1) * MAIN)
                ot[half, lines[b][part], :] = total[:, lanes]
    for half in range(2):
        lanes = slice(half * MAIN, (half + 1) * MAIN)
        bt[:, :, lanes] = ot[half].reshape(OWNERS, PART, MAIN).astype(BF16)
    back_tail = 3, slot(bt), slot(ht)
    keep(back_tail)
    start(back_tail, everyone)
    diagonal = (iota((WIDE, WIDE), 0) // OWNERS == shot_of_point(1)).astype(BF16)
    for b in range(BINS):
        for part, r in enumerate(lines[b]):
            copies = [wide_rows(near, r).astype(BF16)] * SHOTS
            lhs[b, :, part * WIDE : (part + 1) * WIDE] = jnp.concatenate(copies, axis=0) * diagonal

    arrive(2, rm)
    for i in range(POINTS):
        far = rm[lax.div(index(i), SHOTS), lax.rem(index(i), SHOTS)]
        far_main[i * PART : (i + 1) * PART, :] = far.astype(F32)
    for b in range(BINS):
        total = -product(lhs[b], [tile(far_main[r, :].astype(BF16)) for r in lines[b]])
        for s in range(SHOTS):
            for part in range(2):
                om[pl.ds(s * PART + part * BINS + b, OWNERS, stride=SHOTS * PART), :] = total[
                    s * OWNERS : (s + 1) * OWNERS, part * MAIN : (part + 1) * MAIN
                ]
    totals = om[...].reshape(OWNERS, SHOTS, PART, MAIN)
    for k in pairs:
        bm[:, 2 * k : 2 * k + 2] = totals[:, 2 * k : 2 * k + 2].astype(BF16)
        back_main = 4, two(bm, k), two(hm, k)
        keep(back_main)
        start(back_main, everyone)
    arrive(3, ht)
    arrive(4, hm)
    for kind, whole in enumerate((st, sn, sm, bt, bm)):
        sent(kind, whole)


def inverse(hm, ht, table, out, hm_v, ht_v, tab, series, load_sem, store_sem):
    shots = out.shape[0]
    pairs = range(shots // 2)
    loads = [
        pltpu.make_async_copy(table, tab, load_sem.at[0]),
        pltpu.make_async_copy(ht, ht_v, load_sem.at[1]),
        *[
            pltpu.make_async_copy(hm.at[:, pl.ds(2 * k, 2)], hm_v.at[k], load_sem.at[2 + k])
            for k in pairs
        ],
    ]
    for load in loads:
        load.start()
    invert = lambda spectra: dot(spectra, tab[...], ((0,), (0,))).astype(BF16)
    loads[0].wait()
    loads[1].wait()
    series[:, MAIN:, :] = invert(ht_v[...].reshape(2 * F, WIDE)).reshape(shots, TAIL, -1)
    stores = []
    for k in pairs:
        loads[2 + k].wait()
        two = pl.ds(2 * k, 2)
        spectra = [hm_v[k, :, s].reshape(2 * F, MAIN) for s in range(2)]
        series[two, :MAIN, :] = invert(jnp.concatenate(spectra, axis=1)).reshape(2, MAIN, -1)
        stores.append(pltpu.make_async_copy(series.at[two], out.at[two], store_sem.at[k]))
        stores[-1].start()
    for store in stores:
        store.wait()


def shards(traces, surface_point, gather_index):
    shots, receivers, samples = traces.shape
    vmem = lambda *shape, dtype=BF16: pltpu.VMEM(shape, dtype)
    hbm, anywhere = pl.BlockSpec(memory_space=pltpu.HBM), pl.BlockSpec(memory_space=pl.ANY)
    message = lambda lanes: vmem(OWNERS, PART, lanes)
    table = jnp.asarray(dft_rows(samples))
    back = [
        jax.ShapeDtypeStruct((OWNERS, SHOTS, PART, MAIN), BF16),
        jax.ShapeDtypeStruct((OWNERS, PART, WIDE), BF16),
    ]
    spectra = pl.pallas_call(
        kernel,
        out_shape=back,
        in_specs=[hbm] * 4,
        out_specs=[anywhere, anywhere],
        scratch_shapes=[
            pltpu.SMEM((4, 2, 4), jnp.int32),
            pltpu.SMEM((4, 2, 4), jnp.int32),
            vmem(2 * F, samples),
            vmem(SHOTS, receivers // PART, PART, samples),
            vmem(SHOTS * HALF, samples),
            vmem(OWNERS, SHOTS, PART, MAIN),
            message(MAIN),
            message(WIDE),
            vmem(OWNERS, SHOTS, PART, MAIN),
            message(MAIN),
            message(MAIN),
            message(WIDE),
            vmem(2, OWNERS * PART, MAIN, dtype=F32),
            vmem(BINS, WIDE, 2 * WIDE),
            vmem(POINTS * PART, MAIN, dtype=F32),
            vmem(2, POINTS * PART, MAIN, dtype=F32),
            vmem(OWNERS * SHOTS * PART, MAIN, dtype=F32),
            vmem(2, OWNERS * PART, MAIN, dtype=F32),
            vmem(OWNERS, SHOTS, PART, MAIN),
            message(WIDE),
            pltpu.SemaphoreType.DMA((7,)),
            pltpu.SemaphoreType.DMA((2,)),
            pltpu.SemaphoreType.REGULAR((2,)),
            pltpu.SemaphoreType.DMA((5,)),
            pltpu.SemaphoreType.DMA((5,)),
        ],
        compiler_params=pltpu.CompilerParams(
            collective_id=0, has_side_effects=True, vmem_limit_bytes=61 * 2**20
        ),
    )(
        surface_point.transpose(0, 2, 1),
        gather_index.transpose(0, 2, 1),
        traces.reshape(shots, receivers // PART, PART, samples),
        table,
    )
    return pl.pallas_call(
        inverse,
        out_shape=jax.ShapeDtypeStruct((shots, SHARE, samples), BF16),
        in_specs=[anywhere] * 3,
        out_specs=anywhere,
        scratch_shapes=[
            vmem(SHOTS // 2, OWNERS, 2, PART, MAIN),
            message(WIDE),
            vmem(2 * F, samples),
            vmem(SHOTS, SHARE, samples),
            pltpu.SemaphoreType.DMA((2 + SHOTS // 2,)),
            pltpu.SemaphoreType.DMA((SHOTS // 2,)),
        ],
        compiler_params=pltpu.CompilerParams(vmem_limit_bytes=61 * 2**20),
    )(*spectra, table)


def solution(mesh):
    placed = (P("shot", None, None), P(), P())
    return jax.shard_map(
        shards, mesh=mesh, in_specs=placed, out_specs=P("shot", "surf", None), check_vma=False
    )
```

```python
import functools
import math

import jax
import jax.numpy as jnp
import ml_dtypes
import numpy as np
from jax import lax
from jax.experimental import pallas as pl
from jax.experimental.pallas import tpu as pltpu
from jax.sharding import PartitionSpec as P

F = 256
OWNERS = 32
BINS = F // OWNERS
PART = 2 * BINS
SHOTS = 8
POINTS = 32
MAIN, TAIL = 128, 32
SHARE = MAIN + TAIL
HALF = POINTS // 2
WIDE = SHOTS * TAIL
MESH = pl.DeviceIdType.MESH
ROOMS = (4, 6, 8)
F32, BF16 = jnp.float32, jnp.bfloat16


def dft_rows(samples):
    freq = np.arange(F).reshape(OWNERS // 2, BINS, 2).transpose(2, 0, 1).reshape(OWNERS, 1, BINS, 1)
    angles = (freq * np.arange(samples) % samples) * (2.0 * math.pi / samples)
    table = np.concatenate([np.cos(angles), -np.sin(angles)], axis=1)
    table = table.astype(np.float32).astype(ml_dtypes.bfloat16).astype(np.float32)
    scaled = table.reshape(2 * F, samples) * samples**-0.5
    return scaled.astype(ml_dtypes.bfloat16)


def offsets():
    steps = [(z, x, y) for z in range(2) for x in range(4) for y in range(4)][1:]
    return sorted(steps, key=lambda k: -(k[0] + min(k[1], 4 - k[1]) + min(k[2], 4 - k[2])))


def wide_rows(ref, rows):
    return jnp.concatenate([ref[half, rows, :] for half in range(2)], axis=1)


def dot(a, b, contract):
    return lax.dot_general(a, b, (contract, ((), ())), preferred_element_type=F32)


def iota(shape, axis):
    return lax.broadcasted_iota(jnp.int32, shape, axis)


def product(left, right):
    real, imag = right
    both = jnp.concatenate(
        [jnp.concatenate([real, imag], axis=1), jnp.concatenate([-imag, real], axis=1)], axis=0
    )
    return dot(left, both, ((1,), (0,)))


def kernel(
    slots,
    point_ref, gather_ref, traces, table, hm, ht,
    points, gathers, slot_v, slot_of, tab, block, full, xn, sm, sn, st, rm, rn, other, rt,
    near, lhs, far_main, far_tail, om, ot, bm, bt,
    load_sem, pair_sem, send_sem, recv_sem,
):
    group, me = lax.axis_index("surf"), lax.axis_index("shot")
    core = group % 2
    z, x, y = me // 16, (me // 4) % 4, me % 4
    peers = [(z ^ k) * 16 + (x + i) % 4 * 4 + (y + j) % 4 for k, i, j in offsets()]
    away = lambda d: [n for n, step in enumerate(offsets()) if sum(map(bool, step)) == d]
    everyone = away(3) + away(2) + away(1)
    groups = lax.axis_size("surf")

    share = SHARE // PART
    blocks = [pl.ds((group + k) % groups * share, share) for k in range(groups)]
    loads = [
        pltpu.make_async_copy(table, tab, load_sem.at[0]),
        pltpu.make_async_copy(traces.at[:, blocks[0]], block, load_sem.at[1]),
    ]
    for k in range(1, groups):
        part = traces.at[:, blocks[k]], full.at[:, blocks[k]]
        loads.append(pltpu.make_async_copy(*part, load_sem.at[1 + k]))
    loads.append(pltpu.make_async_copy(point_ref, points, load_sem.at[5]))
    loads.append(pltpu.make_async_copy(gather_ref, gathers, load_sem.at[6]))
    for load in loads:
        load.start()
    barrier = pltpu.get_barrier_semaphore()
    pl.semaphore_signal(barrier, inc=1, device_id=(group ^ 1, me), device_id_type=MESH)
    for n in everyone:
        pl.semaphore_signal(barrier, inc=1, device_id=(group, peers[n]), device_id_type=MESH)

    def start(way):
        kind, source, target = way
        pltpu.make_async_copy(source(me), target(me), recv_sem.at[kind]).start()
        for n in everyone:
            pltpu.make_async_remote_copy(
                src_ref=source(peers[n]),
                dst_ref=target(me),
                send_sem=send_sem.at[kind],
                recv_sem=recv_sem.at[kind],
                device_id=(group, peers[n]),
                device_id_type=MESH,
            ).start()

    def arrive(kind, whole):
        pltpu.make_async_copy(whole, whole, recv_sem.at[kind]).wait()

    def sent(kind, whole):
        others = whole.at[pl.ds(0, OWNERS - 1)]
        pltpu.make_async_copy(others, others, send_sem.at[kind]).wait()

    def forward(rows):
        spectra = dot(tab[...], rows, ((1,), (1,))).astype(BF16)
        return spectra.reshape(OWNERS, PART, -1)

    slot = lambda ref: lambda device: ref.at[device]
    two = lambda ref, k: lambda device: ref.at[device, pl.ds(2 * k, 2)]
    rounds = range(slots // 2)
    early = 0 if slots == ROOMS[0] else 1
    pairs = range(SHOTS // 2)
    tail_way, near_way = (0, slot(st), slot(rt)), (1, slot(sn), slot(rn))
    main_ways = [(2, two(sm, k), two(rm, k)) for k in rounds]

    for load in loads[5:]:
        load.wait()
    index = lambda i: gathers[i // 8, i // 4 % 2, i % 4]
    owner = lambda i: lax.div(index(i), SHOTS)
    if slots < SHOTS:
        device = iota((SHOTS, MAIN), 1) * SHOTS + iota((SHOTS, MAIN), 0)
        wanted = jnp.zeros((SHOTS, MAIN), jnp.int32)
        for i in range(POINTS):
            wanted = jnp.where(device == index(i), 1, wanted)
        before = jnp.zeros((1, MAIN), jnp.int32)
        for l in range(SHOTS):
            row = wanted[l : l + 1]
            slot_v[l : l + 1] = before + SHOTS * row
            before = before + row
        table_copy = pltpu.make_async_copy(slot_v, slot_of, load_sem.at[7])
        table_copy.start()
        table_copy.wait()
        mine = [0] * SHOTS
        for l in range(SHOTS):
            for k in range(slots):
                mine[k] = jnp.where(slot_of[l, me] == SHOTS + k, l, mine[k])
        place = lambda i: slot_of[lax.rem(index(i), SHOTS), owner(i)] - SHOTS
    else:
        mine = range(SHOTS)
        place = lambda i: lax.rem(index(i), SHOTS)

    loads[0].wait()
    loads[1].wait()
    spread_own = pltpu.make_async_copy(block, full.at[:, blocks[0]], load_sem.at[8])
    spread_own.start()
    main, tail = pl.ds(0, MAIN // PART), pl.ds(MAIN // PART, TAIL // PART)
    tails = st.shape[2] // TAIL
    rows = [block[mine[k], tail].reshape(TAIL, -1) for k in range(tails)]
    st[...] = forward(jnp.concatenate(rows, axis=0))
    for k in rounds:
        rows = [block[mine[2 * k + j], main].reshape(MAIN, -1) for j in range(2)]
        spectra = forward(jnp.concatenate(rows, axis=0))
        sm[:, 2 * k] = spectra[..., :MAIN]
        sm[:, 2 * k + 1] = spectra[..., MAIN:]

    pl.semaphore_wait(barrier, len(everyone) + 1)
    for way in (tail_way, *main_ways[:early]):
        start(way)

    for load in (*loads[2:5], spread_own):
        load.wait()
    chosen = jnp.zeros((HALF, 1), jnp.int32)
    aligned = []
    for i in range(HALF):
        point = points[core * 2 + i // 8, i // 4 % 2, i % 4]
        aligned.append(lax.div(point, PART))
        chosen = jnp.where(iota((HALF, 1), 0) == i, i * PART + lax.rem(point, PART), chosen)
    pick = (iota((HALF, HALF * PART), 1) == chosen).astype(BF16)
    for s in range(SHOTS):
        rows = jnp.concatenate([full[s, row] for row in aligned], axis=0)
        xn[s * HALF : (s + 1) * HALF, :] = dot(pick, rows, ((1,), (0,))).astype(BF16)
    sn[...] = forward(xn[...])
    for way in (near_way, *main_ways[early:]):
        start(way)

    lines = [[pl.ds(part * BINS + b, OWNERS, stride=PART) for part in range(2)] for b in range(BINS)]
    slot_at = iota((PART, st.shape[2]), 1) // TAIL
    wide = (st.shape[2], WIDE)
    spread = (iota(wide, 0) % TAIL == iota(wide, 1) % TAIL).astype(BF16)
    shot_of_point = lambda axis: iota((WIDE, WIDE), axis) % MAIN // HALF
    tile = lambda a: jnp.concatenate([a[:HALF]] * SHOTS + [a[HALF:]] * SHOTS, axis=0)

    arrive(0, rt)
    picked = []
    for i in range(POINTS):
        picked.append(rt[owner(i)] * (slot_at == place(i)).astype(BF16))
    spectra = dot(jnp.concatenate(picked, axis=0), spread, ((1,), (0,)))
    for half in range(2):
        far_tail[half] = spectra[:, half * MAIN : (half + 1) * MAIN]
    arrive(1, rn)
    swap = pltpu.make_async_remote_copy(
        src_ref=rn,
        dst_ref=other,
        send_sem=pair_sem.at[0],
        recv_sem=pair_sem.at[1],
        device_id=(group ^ 1, me),
        device_id_type=MESH,
    )
    swap.start()
    near[core] = rn[...].reshape(OWNERS * PART, MAIN).astype(F32)
    swap.wait()
    near[1 - core] = other[...].reshape(OWNERS * PART, MAIN).astype(F32)
    diagonal = (shot_of_point(0) == iota((WIDE, WIDE), 1) // TAIL).astype(BF16)
    for b in range(BINS):
        left = jnp.concatenate([wide_rows(near, r).astype(BF16) for r in lines[b]], axis=1)
        right = [tile(wide_rows(far_tail, r).astype(BF16)) * diagonal for r in lines[b]]
        total = -product(left, right)
        for part in range(2):
            for half in range(2):
                lanes = slice(part * WIDE + half * MAIN, part * WIDE + (half + 1) * MAIN)
                ot[half, lines[b][part], :] = total[:, lanes]
    for half in range(2):
        lanes = slice(half * MAIN, (half + 1) * MAIN)
        bt[:, :, lanes] = ot[half].reshape(OWNERS, PART, MAIN).astype(BF16)
    back_tail = 3, slot(bt), slot(ht)
    start(back_tail)
    diagonal = (iota((WIDE, WIDE), 0) // OWNERS == shot_of_point(1)).astype(BF16)
    for b in range(BINS):
        for part, r in enumerate(lines[b]):
            copies = [wide_rows(near, r).astype(BF16)] * SHOTS
            lhs[b, :, part * WIDE : (part + 1) * WIDE] = jnp.concatenate(copies, axis=0) * diagonal

    arrive(2, rm)
    for i in range(POINTS):
        far_main[i * PART : (i + 1) * PART, :] = rm[owner(i), place(i)].astype(F32)
    for b in range(BINS):
        total = -product(lhs[b], [tile(far_main[r, :].astype(BF16)) for r in lines[b]])
        for s in range(SHOTS):
            for part in range(2):
                om[pl.ds(s * PART + part * BINS + b, OWNERS, stride=SHOTS * PART), :] = total[
                    s * OWNERS : (s + 1) * OWNERS, part * MAIN : (part + 1) * MAIN
                ]
    totals = om[...].reshape(OWNERS, SHOTS, PART, MAIN)
    for k in pairs:
        bm[:, 2 * k : 2 * k + 2] = totals[:, 2 * k : 2 * k + 2].astype(BF16)
        back_main = 4, two(bm, k), two(hm, k)
        start(back_main)
    arrive(3, ht)
    arrive(4, hm)
    for kind, whole in enumerate((st, sn, sm, bt, bm)):
        sent(kind, whole)


def inverse(hm, ht, table, out, hm_v, ht_v, tab, series, load_sem, store_sem):
    shots, _, samples = out.shape
    pairs = range(shots // 2)
    loads = [
        pltpu.make_async_copy(table, tab, load_sem.at[0]),
        pltpu.make_async_copy(ht, ht_v, load_sem.at[1]),
        *[
            pltpu.make_async_copy(hm.at[:, pl.ds(2 * k, 2)], hm_v.at[k], load_sem.at[2 + k])
            for k in pairs
        ],
    ]
    for load in loads:
        load.start()

    def invert(spectra, two, receivers):
        even = dot(spectra[:F], tab[:F], ((0,), (0,)))
        odd = dot(spectra[F:], tab[F:], ((0,), (0,)))
        shape = (two.stop - two.start, receivers.stop - receivers.start, samples // 2)
        series[two, receivers, : samples // 2] = (even + odd).astype(BF16).reshape(shape)
        series[two, receivers, samples // 2 :] = (even - odd).astype(BF16).reshape(shape)

    loads[0].wait()
    loads[1].wait()
    invert(ht_v[...].reshape(2 * F, WIDE), slice(0, shots), slice(MAIN, SHARE))
    stores = []
    for k in pairs:
        loads[2 + k].wait()
        two = pl.ds(2 * k, 2)
        spectra = [hm_v[k, :, s].reshape(2 * F, MAIN) for s in range(2)]
        invert(jnp.concatenate(spectra, axis=1), slice(2 * k, 2 * k + 2), slice(0, MAIN))
        stores.append(pltpu.make_async_copy(series.at[two], out.at[two], store_sem.at[k]))
        stores[-1].start()
    for store in stores:
        store.wait()


def tail_lanes(slots):
    return MAIN if slots * TAIL <= MAIN else WIDE


def shards(traces, surface_point, gather_index):
    shots, receivers, samples = traces.shape
    vmem = lambda *shape, dtype=BF16: pltpu.VMEM(shape, dtype)
    hbm, anywhere = pl.BlockSpec(memory_space=pltpu.HBM), pl.BlockSpec(memory_space=pl.ANY)
    message = lambda lanes: vmem(OWNERS, PART, lanes)
    table = dft_rows(samples)
    back = [
        jax.ShapeDtypeStruct((OWNERS, SHOTS, PART, MAIN), BF16),
        jax.ShapeDtypeStruct((OWNERS, PART, WIDE), BF16),
    ]
    product = lambda slots: pl.pallas_call(
        functools.partial(kernel, slots),
        out_shape=back,
        in_specs=[hbm] * 4,
        out_specs=[anywhere, anywhere],
        scratch_shapes=[
            pltpu.SMEM((4, 2, 4), jnp.int32),
            pltpu.SMEM((4, 2, 4), jnp.int32),
            vmem(SHOTS, MAIN, dtype=jnp.int32),
            pltpu.SMEM((SHOTS, MAIN), jnp.int32),
            vmem(2 * F, samples),
            vmem(SHOTS, SHARE // PART, PART, samples),
            vmem(SHOTS, receivers // PART, PART, samples),
            vmem(SHOTS * HALF, samples),
            vmem(OWNERS, slots, PART, MAIN),
            message(MAIN),
            message(tail_lanes(slots)),
            vmem(OWNERS, slots, PART, MAIN),
            message(MAIN),
            message(MAIN),
            message(tail_lanes(slots)),
            vmem(2, OWNERS * PART, MAIN, dtype=F32),
            vmem(BINS, WIDE, 2 * WIDE),
            vmem(POINTS * PART, MAIN, dtype=F32),
            vmem(2, POINTS * PART, MAIN, dtype=F32),
            vmem(OWNERS * SHOTS * PART, MAIN, dtype=F32),
            vmem(2, OWNERS * PART, MAIN, dtype=F32),
            vmem(OWNERS, SHOTS, PART, MAIN),
            message(WIDE),
            pltpu.SemaphoreType.DMA((9,)),
            pltpu.SemaphoreType.DMA((2,)),
            pltpu.SemaphoreType.DMA((5,)),
            pltpu.SemaphoreType.DMA((5,)),
        ],
        compiler_params=pltpu.CompilerParams(
            collective_id=slots // 2, has_side_effects=True, vmem_limit_bytes=61 * 2**20
        ),
    )
    points, gathers = surface_point.transpose(0, 2, 1), gather_index.transpose(0, 2, 1)
    blocks = traces.reshape(shots, receivers // PART, PART, samples)
    numbers = jnp.arange(OWNERS * SHOTS, dtype=jnp.int32).reshape(OWNERS, SHOTS)
    wanted = jnp.any(gathers[..., None, None] == numbers, axis=(0, 1, 2))
    most = jnp.max(jnp.sum(wanted.astype(jnp.int32), axis=1))
    case = sum((most > room).astype(jnp.int32) for room in ROOMS[:-1])
    spectra = lax.switch(case, [product(room) for room in ROOMS], points, gathers, blocks, jnp.asarray(table))
    return pl.pallas_call(
        inverse,
        out_shape=jax.ShapeDtypeStruct((shots, SHARE, samples), BF16),
        in_specs=[anywhere] * 3,
        out_specs=anywhere,
        scratch_shapes=[
            vmem(SHOTS // 2, OWNERS, 2, PART, MAIN),
            message(WIDE),
            vmem(2 * F, samples // 2),
            vmem(SHOTS, SHARE, samples),
            pltpu.SemaphoreType.DMA((2 + SHOTS // 2,)),
            pltpu.SemaphoreType.DMA((SHOTS // 2,)),
        ],
        compiler_params=pltpu.CompilerParams(vmem_limit_bytes=61 * 2**20),
    )(*spectra, jnp.asarray(table[:, : samples // 2]))


def solution(mesh):
    placed = (P("shot", None, None), P(), P())
    return jax.shard_map(
        shards, mesh=mesh, in_specs=placed, out_specs=P("shot", "surf", None), check_vma=False
    )
```

```python
import functools
import math

import jax
import jax.numpy as jnp
import ml_dtypes
import numpy as np
from jax import lax
from jax.experimental import pallas as pl
from jax.experimental.pallas import tpu as pltpu
from jax.sharding import PartitionSpec as P

F = 256
OWNERS = 32
BINS = F // OWNERS
PART = 2 * BINS
SHOTS = 8
POINTS = 32
MAIN, TAIL = 128, 32
SHARE = MAIN + TAIL
HALF = POINTS // 2
WIDE = SHOTS * TAIL
MESH = pl.DeviceIdType.MESH
ROOMS = (4, 6, 8)
F32, BF16 = jnp.float32, jnp.bfloat16


def dft_rows(samples):
    freq = np.arange(F).reshape(OWNERS // 2, BINS, 2).transpose(2, 0, 1).reshape(OWNERS, 1, BINS, 1)
    angles = (freq * np.arange(samples) % samples) * (2.0 * math.pi / samples)
    table = np.concatenate([np.cos(angles), -np.sin(angles)], axis=1)
    table = table.astype(np.float32).astype(ml_dtypes.bfloat16).astype(np.float32)
    scaled = table.reshape(2 * F, samples) * samples**-0.5
    return scaled.astype(ml_dtypes.bfloat16)


def offsets():
    steps = [(z, x, y) for z in range(2) for x in range(4) for y in range(4)][1:]
    return sorted(steps, key=lambda k: -(k[0] + min(k[1], 4 - k[1]) + min(k[2], 4 - k[2])))


def wide_rows(ref, rows):
    return jnp.concatenate([ref[half, rows, :] for half in range(2)], axis=1)


def dot(a, b, contract):
    return lax.dot_general(a, b, (contract, ((), ())), preferred_element_type=F32)


def iota(shape, axis):
    return lax.broadcasted_iota(jnp.int32, shape, axis)


def product(left, right):
    real, imag = right
    both = jnp.concatenate(
        [jnp.concatenate([real, imag], axis=1), jnp.concatenate([-imag, real], axis=1)], axis=0
    )
    return dot(left, both, ((1,), (0,)))


def kernel(
    slots,
    point_ref, gather_ref, traces, table, hm, ht,
    points, gathers, slot_v, slot_of, tab, block, full, xn, sm, sn, st, rm, rn, other, rt,
    near, lhs, far_main, far_tail, om, ot, bm, bt,
    load_sem, pair_sem, send_sem, recv_sem,
):
    group, me = lax.axis_index("surf"), lax.axis_index("shot")
    core = group % 2
    z, x, y = me // 16, (me // 4) % 4, me % 4
    peers = [(z ^ k) * 16 + (x + i) % 4 * 4 + (y + j) % 4 for k, i, j in offsets()]
    away = lambda d: [n for n, step in enumerate(offsets()) if sum(map(bool, step)) == d]
    everyone = away(3) + away(2) + away(1)
    groups = lax.axis_size("surf")

    share = SHARE // PART
    blocks = [pl.ds((group + k) % groups * share, share) for k in range(groups)]
    loads = [
        pltpu.make_async_copy(table, tab, load_sem.at[0]),
        pltpu.make_async_copy(traces.at[:, blocks[0]], block, load_sem.at[1]),
    ]
    for k in range(1, groups):
        part = traces.at[:, blocks[k]], full.at[:, blocks[k]]
        loads.append(pltpu.make_async_copy(*part, load_sem.at[1 + k]))
    loads.append(pltpu.make_async_copy(point_ref, points, load_sem.at[5]))
    loads.append(pltpu.make_async_copy(gather_ref, gathers, load_sem.at[6]))
    for load in loads:
        load.start()
    barrier = pltpu.get_barrier_semaphore()
    pl.semaphore_signal(barrier, inc=1, device_id=(group ^ 1, me), device_id_type=MESH)
    for n in everyone:
        pl.semaphore_signal(barrier, inc=1, device_id=(group, peers[n]), device_id_type=MESH)

    def start(way):
        kind, source, target = way
        pltpu.make_async_copy(source(me), target(me), recv_sem.at[kind]).start()
        for n in everyone:
            pltpu.make_async_remote_copy(
                src_ref=source(peers[n]),
                dst_ref=target(me),
                send_sem=send_sem.at[kind],
                recv_sem=recv_sem.at[kind],
                device_id=(group, peers[n]),
                device_id_type=MESH,
            ).start()

    def arrive(kind, whole):
        pltpu.make_async_copy(whole, whole, recv_sem.at[kind]).wait()

    def sent(kind, whole):
        others = whole.at[pl.ds(0, OWNERS - 1)]
        pltpu.make_async_copy(others, others, send_sem.at[kind]).wait()

    def forward(rows):
        spectra = dot(tab[...], rows, ((1,), (1,))).astype(BF16)
        return spectra.reshape(OWNERS, PART, -1)

    slot = lambda ref: lambda device: ref.at[device]
    two = lambda ref, k: lambda device: ref.at[device, pl.ds(2 * k, 2)]
    rounds = range(slots // 2)
    early = 0 if slots == ROOMS[0] else 1
    pairs = range(SHOTS // 2)
    tail_way, near_way = (0, slot(st), slot(rt)), (1, slot(sn), slot(rn))
    main_ways = [(2, two(sm, k), two(rm, k)) for k in rounds]

    for load in loads[5:]:
        load.wait()
    index = lambda i: gathers[i // 8, i // 4 % 2, i % 4]
    owner = lambda i: lax.div(index(i), SHOTS)
    if slots < SHOTS:
        wanted = wanted_of(index)
        before = jnp.zeros((1, MAIN), jnp.int32)
        for l in range(SHOTS):
            row = wanted[l : l + 1]
            slot_v[l : l + 1] = before + SHOTS * row
            before = before + row
        table_copy = pltpu.make_async_copy(slot_v, slot_of, load_sem.at[7])
        table_copy.start()
        table_copy.wait()
        mine = [0] * SHOTS
        for l in range(SHOTS):
            for k in range(slots):
                mine[k] = jnp.where(slot_of[l, me] == SHOTS + k, l, mine[k])
        place = lambda i: slot_of[lax.rem(index(i), SHOTS), owner(i)] - SHOTS
    else:
        mine = range(SHOTS)
        place = lambda i: lax.rem(index(i), SHOTS)

    loads[0].wait()
    loads[1].wait()
    spread_own = pltpu.make_async_copy(block, full.at[:, blocks[0]], load_sem.at[8])
    spread_own.start()
    main, tail = pl.ds(0, MAIN // PART), pl.ds(MAIN // PART, TAIL // PART)
    tails = st.shape[2] // TAIL
    rows = [block[mine[k], tail].reshape(TAIL, -1) for k in range(tails)]
    st[...] = forward(jnp.concatenate(rows, axis=0))
    for k in rounds:
        rows = [block[mine[2 * k + j], main].reshape(MAIN, -1) for j in range(2)]
        spectra = forward(jnp.concatenate(rows, axis=0))
        sm[:, 2 * k] = spectra[..., :MAIN]
        sm[:, 2 * k + 1] = spectra[..., MAIN:]

    pl.semaphore_wait(barrier, len(everyone) + 1)
    for way in (tail_way, *main_ways[:early]):
        start(way)

    for load in (*loads[2:5], spread_own):
        load.wait()
    chosen = jnp.zeros((HALF, 1), jnp.int32)
    aligned = []
    for i in range(HALF):
        point = points[core * 2 + i // 8, i // 4 % 2, i % 4]
        aligned.append(lax.div(point, PART))
        chosen = jnp.where(iota((HALF, 1), 0) == i, i * PART + lax.rem(point, PART), chosen)
    pick = (iota((HALF, HALF * PART), 1) == chosen).astype(BF16)
    for s in range(SHOTS):
        rows = jnp.concatenate([full[s, row] for row in aligned], axis=0)
        xn[s * HALF : (s + 1) * HALF, :] = dot(pick, rows, ((1,), (0,))).astype(BF16)
    sn[...] = forward(xn[...])
    for way in (near_way, *main_ways[early:]):
        start(way)

    lines = [[pl.ds(part * BINS + b, OWNERS, stride=PART) for part in range(2)] for b in range(BINS)]
    slot_at = iota((PART, st.shape[2]), 1) // TAIL
    wide = (st.shape[2], WIDE)
    spread = (iota(wide, 0) % TAIL == iota(wide, 1) % TAIL).astype(BF16)
    shot_of_point = lambda axis: iota((WIDE, WIDE), axis) % MAIN // HALF
    tile = lambda a: jnp.concatenate([a[:HALF]] * SHOTS + [a[HALF:]] * SHOTS, axis=0)

    arrive(0, rt)
    picked = []
    for i in range(POINTS):
        picked.append(rt[owner(i)] * (slot_at == place(i)).astype(BF16))
    spectra = dot(jnp.concatenate(picked, axis=0), spread, ((1,), (0,)))
    for half in range(2):
        far_tail[half] = spectra[:, half * MAIN : (half + 1) * MAIN]
    arrive(1, rn)
    swap = pltpu.make_async_remote_copy(
        src_ref=rn,
        dst_ref=other,
        send_sem=pair_sem.at[0],
        recv_sem=pair_sem.at[1],
        device_id=(group ^ 1, me),
        device_id_type=MESH,
    )
    swap.start()
    near[core] = rn[...].reshape(OWNERS * PART, MAIN).astype(F32)
    swap.wait()
    near[1 - core] = other[...].reshape(OWNERS * PART, MAIN).astype(F32)
    diagonal = (shot_of_point(0) == iota((WIDE, WIDE), 1) // TAIL).astype(BF16)
    for b in range(BINS):
        left = jnp.concatenate([wide_rows(near, r).astype(BF16) for r in lines[b]], axis=1)
        right = [tile(wide_rows(far_tail, r).astype(BF16)) * diagonal for r in lines[b]]
        total = -product(left, right)
        for part in range(2):
            for half in range(2):
                lanes = slice(part * WIDE + half * MAIN, part * WIDE + (half + 1) * MAIN)
                ot[half, lines[b][part], :] = total[:, lanes]
    for half in range(2):
        lanes = slice(half * MAIN, (half + 1) * MAIN)
        bt[:, :, lanes] = ot[half].reshape(OWNERS, PART, MAIN).astype(BF16)
    back_tail = 3, slot(bt), slot(ht)
    start(back_tail)
    diagonal = (iota((WIDE, WIDE), 0) // OWNERS == shot_of_point(1)).astype(BF16)
    for b in range(BINS):
        for part, r in enumerate(lines[b]):
            copies = [wide_rows(near, r).astype(BF16)] * SHOTS
            lhs[b, :, part * WIDE : (part + 1) * WIDE] = jnp.concatenate(copies, axis=0) * diagonal

    arrive(2, rm)
    for i in range(POINTS):
        far_main[i * PART : (i + 1) * PART, :] = rm[owner(i), place(i)].astype(F32)
    for b in range(BINS):
        total = -product(lhs[b], [tile(far_main[r, :].astype(BF16)) for r in lines[b]])
        for s in range(SHOTS):
            for part in range(2):
                om[pl.ds(s * PART + part * BINS + b, OWNERS, stride=SHOTS * PART), :] = total[
                    s * OWNERS : (s + 1) * OWNERS, part * MAIN : (part + 1) * MAIN
                ]
    totals = om[...].reshape(OWNERS, SHOTS, PART, MAIN)
    for k in pairs:
        bm[:, 2 * k : 2 * k + 2] = totals[:, 2 * k : 2 * k + 2].astype(BF16)
        back_main = 4, two(bm, k), two(hm, k)
        start(back_main)
    arrive(3, ht)
    arrive(4, hm)
    for kind, whole in enumerate((st, sn, sm, bt, bm)):
        sent(kind, whole)


def wanted_of(index):
    gather = iota((SHOTS, MAIN), 1) * SHOTS + iota((SHOTS, MAIN), 0)
    wanted = jnp.zeros((SHOTS, MAIN), jnp.int32)
    for i in range(POINTS):
        wanted = jnp.where(gather == index(i), 1, wanted)
    return wanted


def choose(gathers, case):
    wanted = wanted_of(lambda i: gathers[i // 8, i // 4 % 2, i % 4])
    most = jnp.max(jnp.sum(wanted, axis=0, keepdims=True))
    case[0] = sum((most > room).astype(jnp.int32) for room in ROOMS[:-1])


def inverse(hm, ht, tab, out, series, store_sem):
    shots, _, samples = out.shape
    pairs = range(shots // 2)
    def invert(spectra, two, receivers):
        even = dot(spectra[:F], tab[:F], ((0,), (0,)))
        odd = dot(spectra[F:], tab[F:], ((0,), (0,)))
        shape = (two.stop - two.start, receivers.stop - receivers.start, samples // 2)
        series[two, receivers, : samples // 2] = (even + odd).astype(BF16).reshape(shape)
        series[two, receivers, samples // 2 :] = (even - odd).astype(BF16).reshape(shape)

    invert(ht[...].reshape(2 * F, WIDE), slice(0, shots), slice(MAIN, SHARE))
    stores = []
    for k in pairs:
        two = pl.ds(2 * k, 2)
        spectra = [hm[:, 2 * k + s].reshape(2 * F, MAIN) for s in range(2)]
        invert(jnp.concatenate(spectra, axis=1), slice(2 * k, 2 * k + 2), slice(0, MAIN))
        stores.append(pltpu.make_async_copy(series.at[two], out.at[two], store_sem.at[k]))
        stores[-1].start()
    for store in stores:
        store.wait()


def tail_lanes(slots):
    return MAIN if slots * TAIL <= MAIN else WIDE


def shards(traces, surface_point, gather_index):
    shots, receivers, samples = traces.shape
    vmem = lambda *shape, dtype=BF16: pltpu.VMEM(shape, dtype)
    hbm, anywhere = pl.BlockSpec(memory_space=pltpu.HBM), pl.BlockSpec(memory_space=pl.ANY)
    message = lambda lanes: vmem(OWNERS, PART, lanes)
    table = dft_rows(samples)
    back = [
        jax.ShapeDtypeStruct((OWNERS, SHOTS, PART, MAIN), BF16),
        jax.ShapeDtypeStruct((OWNERS, PART, WIDE), BF16),
    ]
    product = lambda slots: pl.pallas_call(
        functools.partial(kernel, slots),
        out_shape=back,
        in_specs=[hbm] * 4,
        out_specs=[anywhere, anywhere],
        scratch_shapes=[
            pltpu.SMEM((4, 2, 4), jnp.int32),
            pltpu.SMEM((4, 2, 4), jnp.int32),
            vmem(SHOTS, MAIN, dtype=jnp.int32),
            pltpu.SMEM((SHOTS, MAIN), jnp.int32),
            vmem(2 * F, samples),
            vmem(SHOTS, SHARE // PART, PART, samples),
            vmem(SHOTS, receivers // PART, PART, samples),
            vmem(SHOTS * HALF, samples),
            vmem(OWNERS, slots, PART, MAIN),
            message(MAIN),
            message(tail_lanes(slots)),
            vmem(OWNERS, slots, PART, MAIN),
            message(MAIN),
            message(MAIN),
            message(tail_lanes(slots)),
            vmem(2, OWNERS * PART, MAIN, dtype=F32),
            vmem(BINS, WIDE, 2 * WIDE),
            vmem(POINTS * PART, MAIN, dtype=F32),
            vmem(2, POINTS * PART, MAIN, dtype=F32),
            vmem(OWNERS * SHOTS * PART, MAIN, dtype=F32),
            vmem(2, OWNERS * PART, MAIN, dtype=F32),
            vmem(OWNERS, SHOTS, PART, MAIN),
            message(WIDE),
            pltpu.SemaphoreType.DMA((9,)),
            pltpu.SemaphoreType.DMA((2,)),
            pltpu.SemaphoreType.DMA((5,)),
            pltpu.SemaphoreType.DMA((5,)),
        ],
        compiler_params=pltpu.CompilerParams(
            collective_id=slots // 2, has_side_effects=True, vmem_limit_bytes=50 * 2**20
        ),
    )
    points, gathers = surface_point.transpose(0, 2, 1), gather_index.transpose(0, 2, 1)
    blocks = traces.reshape(shots, receivers // PART, PART, samples)
    case = pl.pallas_call(
        choose,
        out_shape=jax.ShapeDtypeStruct((1,), jnp.int32),
        in_specs=[pl.BlockSpec(memory_space=pltpu.SMEM)],
        out_specs=pl.BlockSpec(memory_space=pltpu.SMEM),
    )(gathers)[0]
    spectra = lax.switch(case, [product(room) for room in ROOMS], points, gathers, blocks, jnp.asarray(table))
    return pl.pallas_call(
        inverse,
        out_shape=jax.ShapeDtypeStruct((shots, SHARE, samples), BF16),
        in_specs=[pl.BlockSpec(memory_space=pltpu.VMEM)] * 3,
        out_specs=anywhere,
        scratch_shapes=[
            vmem(SHOTS, SHARE, samples),
            pltpu.SemaphoreType.DMA((SHOTS // 2,)),
        ],
        compiler_params=pltpu.CompilerParams(vmem_limit_bytes=50 * 2**20),
    )(*spectra, jnp.asarray(table[:, : samples // 2]))


def solution(mesh):
    placed = (P("shot", None, None), P(), P())
    return jax.shard_map(
        shards, mesh=mesh, in_specs=placed, out_specs=P("shot", "surf", None), check_vma=False
    )
```

```python
import functools
import math

import jax
import jax.numpy as jnp
import ml_dtypes
import numpy as np
from jax import lax
from jax.experimental import pallas as pl
from jax.experimental.pallas import tpu as pltpu
from jax.sharding import PartitionSpec as P

F = 256
OWNERS = 32
BINS = F // OWNERS
PART = 2 * BINS
SHOTS = 8
POINTS = 32
MAIN, TAIL = 128, 32
SHARE = MAIN + TAIL
HALF = POINTS // 2
WIDE = SHOTS * TAIL
MESH = pl.DeviceIdType.MESH
ROOMS = (4, 6, 8)
F32, BF16 = jnp.float32, jnp.bfloat16


def dft_rows(samples):
    freq = np.arange(F).reshape(OWNERS // 2, BINS, 2).transpose(2, 0, 1).reshape(OWNERS, 1, BINS, 1)
    angles = (freq * np.arange(samples) % samples) * (2.0 * math.pi / samples)
    table = np.concatenate([np.cos(angles), -np.sin(angles)], axis=1)
    table = table.astype(np.float32).astype(ml_dtypes.bfloat16).astype(np.float32)
    scaled = table.reshape(2 * F, samples) * samples**-0.5
    return scaled.astype(ml_dtypes.bfloat16)


def offsets():
    steps = [(z, x, y) for z in range(2) for x in range(4) for y in range(4)][1:]
    return sorted(steps, key=lambda k: -(k[0] + min(k[1], 4 - k[1]) + min(k[2], 4 - k[2])))


def wide_rows(ref, rows):
    return jnp.concatenate([ref[half, rows, :] for half in range(2)], axis=1)


def dot(a, b, contract):
    return lax.dot_general(a, b, (contract, ((), ())), preferred_element_type=F32)


def iota(shape, axis):
    return lax.broadcasted_iota(jnp.int32, shape, axis)


def product(left, right):
    real, imag = right
    both = jnp.concatenate(
        [jnp.concatenate([real, imag], axis=1), jnp.concatenate([-imag, real], axis=1)], axis=0
    )
    return dot(left, both, ((1,), (0,)))


def kernel(
    slots,
    point_ref, gather_ref, traces, table, hm, ht,
    points, gathers, slot_v, slot_of, tab, block, full, xn, sm, sn, st, rm, rn, other, rt,
    near, lhs, far_main, far_tail, om, ot, bm, bt,
    load_sem, pair_sem, send_sem, recv_sem,
):
    group, me = lax.axis_index("surf"), lax.axis_index("shot")
    core = group % 2
    z, x, y = me // 16, (me // 4) % 4, me % 4
    peers = [(z ^ k) * 16 + (x + i) % 4 * 4 + (y + j) % 4 for k, i, j in offsets()]
    away = lambda d: [n for n, step in enumerate(offsets()) if sum(map(bool, step)) == d]
    everyone = away(3) + away(2) + away(1)
    groups = lax.axis_size("surf")

    share = SHARE // PART
    blocks = [pl.ds((group + k) % groups * share, share) for k in range(groups)]
    loads = [
        pltpu.make_async_copy(table, tab, load_sem.at[0]),
        pltpu.make_async_copy(traces.at[:, blocks[0]], block, load_sem.at[1]),
    ]
    for k in range(1, groups):
        part = traces.at[:, blocks[k]], full.at[:, blocks[k]]
        loads.append(pltpu.make_async_copy(*part, load_sem.at[1 + k]))
    loads.append(pltpu.make_async_copy(point_ref, points, load_sem.at[5]))
    loads.append(pltpu.make_async_copy(gather_ref, gathers, load_sem.at[6]))
    for load in loads:
        load.start()
    barrier = pltpu.get_barrier_semaphore()
    pl.semaphore_signal(barrier, inc=1, device_id=(group ^ 1, me), device_id_type=MESH)
    for n in everyone:
        pl.semaphore_signal(barrier, inc=1, device_id=(group, peers[n]), device_id_type=MESH)

    def start(way):
        kind, source, target = way
        pltpu.make_async_copy(source(me), target(me), recv_sem.at[kind]).start()
        for n in everyone:
            pltpu.make_async_remote_copy(
                src_ref=source(peers[n]),
                dst_ref=target(me),
                send_sem=send_sem.at[kind],
                recv_sem=recv_sem.at[kind],
                device_id=(group, peers[n]),
                device_id_type=MESH,
            ).start()

    def arrive(kind, whole):
        pltpu.make_async_copy(whole, whole, recv_sem.at[kind]).wait()

    def sent(kind, whole):
        others = whole.at[pl.ds(0, OWNERS - 1)]
        pltpu.make_async_copy(others, others, send_sem.at[kind]).wait()

    def forward(rows):
        spectra = dot(tab[...], rows, ((1,), (1,))).astype(BF16)
        return spectra.reshape(OWNERS, PART, -1)

    slot = lambda ref: lambda device: ref.at[device]
    two = lambda ref, k: lambda device: ref.at[device, pl.ds(2 * k, 2)]
    rounds = range(slots // 2)
    early = 0 if slots == ROOMS[0] else 1
    pairs = range(SHOTS // 2)
    tail_way, near_way = (0, slot(st), slot(rt)), (1, slot(sn), slot(rn))
    main_ways = [(2, two(sm, k), two(rm, k)) for k in rounds]

    for load in loads[5:]:
        load.wait()
    index = lambda i: gathers[i // 8, i // 4 % 2, i % 4]
    owner = lambda i: lax.div(index(i), SHOTS)
    if slots < SHOTS:
        wanted = wanted_of(index)
        before = jnp.zeros((1, MAIN), jnp.int32)
        for l in range(SHOTS):
            row = wanted[l : l + 1]
            slot_v[l : l + 1] = before + SHOTS * row
            before = before + row
        table_copy = pltpu.make_async_copy(slot_v, slot_of, load_sem.at[7])
        table_copy.start()
        table_copy.wait()
        mine = [0] * SHOTS
        for l in range(SHOTS):
            for k in range(slots):
                mine[k] = jnp.where(slot_of[l, me] == SHOTS + k, l, mine[k])
        place = lambda i: slot_of[lax.rem(index(i), SHOTS), owner(i)] - SHOTS
    else:
        mine = range(SHOTS)
        place = lambda i: lax.rem(index(i), SHOTS)

    loads[0].wait()
    loads[1].wait()
    spread_own = pltpu.make_async_copy(block, full.at[:, blocks[0]], load_sem.at[8])
    spread_own.start()
    main, tail = pl.ds(0, MAIN // PART), pl.ds(MAIN // PART, TAIL // PART)
    tails = st.shape[2] // TAIL
    rows = [block[mine[k], tail].reshape(TAIL, -1) for k in range(tails)]
    st[...] = forward(jnp.concatenate(rows, axis=0))
    for k in rounds:
        rows = [block[mine[2 * k + j], main].reshape(MAIN, -1) for j in range(2)]
        spectra = forward(jnp.concatenate(rows, axis=0))
        sm[:, 2 * k] = spectra[..., :MAIN]
        sm[:, 2 * k + 1] = spectra[..., MAIN:]

    pl.semaphore_wait(barrier, len(everyone) + 1)
    for way in (tail_way, *main_ways[:early]):
        start(way)

    for load in (*loads[2:5], spread_own):
        load.wait()
    chosen = jnp.zeros((HALF, 1), jnp.int32)
    aligned = []
    for i in range(HALF):
        point = points[core * 2 + i // 8, i // 4 % 2, i % 4]
        aligned.append(lax.div(point, PART))
        chosen = jnp.where(iota((HALF, 1), 0) == i, i * PART + lax.rem(point, PART), chosen)
    pick = (iota((HALF, HALF * PART), 1) == chosen).astype(BF16)
    for s in range(SHOTS):
        rows = jnp.concatenate([full[s, row] for row in aligned], axis=0)
        xn[s * HALF : (s + 1) * HALF, :] = dot(pick, rows, ((1,), (0,))).astype(BF16)
    sn[...] = forward(xn[...])
    for way in (near_way, *main_ways[early:]):
        start(way)

    lines = [[pl.ds(part * BINS + b, OWNERS, stride=PART) for part in range(2)] for b in range(BINS)]
    slot_at = iota((PART, st.shape[2]), 1) // TAIL
    wide = (st.shape[2], WIDE)
    spread = (iota(wide, 0) % TAIL == iota(wide, 1) % TAIL).astype(BF16)
    shot_of_point = lambda axis: iota((WIDE, WIDE), axis) % MAIN // HALF
    tile = lambda a: jnp.concatenate([a[:HALF]] * SHOTS + [a[HALF:]] * SHOTS, axis=0)

    arrive(0, rt)
    picked = []
    for i in range(POINTS):
        picked.append(rt[owner(i)] * (slot_at == place(i)).astype(BF16))
    spectra = dot(jnp.concatenate(picked, axis=0), spread, ((1,), (0,)))
    for half in range(2):
        far_tail[half] = spectra[:, half * MAIN : (half + 1) * MAIN]
    arrive(1, rn)
    swap = pltpu.make_async_remote_copy(
        src_ref=rn,
        dst_ref=other,
        send_sem=pair_sem.at[0],
        recv_sem=pair_sem.at[1],
        device_id=(group ^ 1, me),
        device_id_type=MESH,
    )
    swap.start()
    near[core] = rn[...].reshape(OWNERS * PART, MAIN).astype(F32)
    swap.wait()
    near[1 - core] = other[...].reshape(OWNERS * PART, MAIN).astype(F32)
    diagonal = (shot_of_point(0) == iota((WIDE, WIDE), 1) // TAIL).astype(BF16)
    for b in range(BINS):
        left = jnp.concatenate([wide_rows(near, r).astype(BF16) for r in lines[b]], axis=1)
        right = [tile(wide_rows(far_tail, r).astype(BF16)) * diagonal for r in lines[b]]
        total = -product(left, right)
        for part in range(2):
            for half in range(2):
                lanes = slice(part * WIDE + half * MAIN, part * WIDE + (half + 1) * MAIN)
                ot[half, lines[b][part], :] = total[:, lanes]
    for half in range(2):
        lanes = slice(half * MAIN, (half + 1) * MAIN)
        bt[:, :, lanes] = ot[half].reshape(OWNERS, PART, MAIN).astype(BF16)
    back_tail = 3, slot(bt), slot(ht)
    start(back_tail)
    diagonal = (iota((WIDE, WIDE), 0) // OWNERS == shot_of_point(1)).astype(BF16)
    for b in range(BINS):
        for part, r in enumerate(lines[b]):
            copies = [wide_rows(near, r).astype(BF16)] * SHOTS
            lhs[b, :, part * WIDE : (part + 1) * WIDE] = jnp.concatenate(copies, axis=0) * diagonal

    arrive(2, rm)
    for i in range(POINTS):
        far_main[i * PART : (i + 1) * PART, :] = rm[owner(i), place(i)].astype(F32)
    for b in range(BINS):
        total = -product(lhs[b], [tile(far_main[r, :].astype(BF16)) for r in lines[b]])
        for s in range(SHOTS):
            for part in range(2):
                om[pl.ds(s * PART + part * BINS + b, OWNERS, stride=SHOTS * PART), :] = total[
                    s * OWNERS : (s + 1) * OWNERS, part * MAIN : (part + 1) * MAIN
                ]
    totals = om[...].reshape(OWNERS, SHOTS, PART, MAIN)
    four = lambda ref, k: lambda device: ref.at[device, pl.ds(4 * k, 4)]
    for k in range(2):
        bm[:, 4 * k : 4 * k + 4] = totals[:, 4 * k : 4 * k + 4].astype(BF16)
        back_main = 4, four(bm, k), four(hm, k)
        start(back_main)
    arrive(3, ht)
    arrive(4, hm)
    for kind, whole in enumerate((st, sn, sm, bt, bm)):
        sent(kind, whole)


def wanted_of(index):
    gather = iota((SHOTS, MAIN), 1) * SHOTS + iota((SHOTS, MAIN), 0)
    wanted = jnp.zeros((SHOTS, MAIN), jnp.int32)
    for i in range(POINTS):
        wanted = jnp.where(gather == index(i), 1, wanted)
    return wanted


def choose(gathers, case):
    wanted = wanted_of(lambda i: gathers[i // 8, i // 4 % 2, i % 4])
    most = jnp.max(jnp.sum(wanted, axis=0, keepdims=True))
    case[0] = sum((most > room).astype(jnp.int32) for room in ROOMS[:-1])


def inverse(hm, ht, tab, out, series, store_sem):
    shots, _, samples = out.shape
    pairs = range(shots // 2)
    def invert(spectra, two, receivers):
        even = dot(spectra[:F], tab[:F], ((0,), (0,)))
        odd = dot(spectra[F:], tab[F:], ((0,), (0,)))
        shape = (two.stop - two.start, receivers.stop - receivers.start, samples // 2)
        series[two, receivers, : samples // 2] = (even + odd).astype(BF16).reshape(shape)
        series[two, receivers, samples // 2 :] = (even - odd).astype(BF16).reshape(shape)

    invert(ht[...].reshape(2 * F, WIDE), slice(0, shots), slice(MAIN, SHARE))
    stores = []
    for k in pairs:
        two = pl.ds(2 * k, 2)
        spectra = [hm[:, 2 * k + s].reshape(2 * F, MAIN) for s in range(2)]
        invert(jnp.concatenate(spectra, axis=1), slice(2 * k, 2 * k + 2), slice(0, MAIN))
        stores.append(pltpu.make_async_copy(series.at[two], out.at[two], store_sem.at[k]))
        stores[-1].start()
    for store in stores:
        store.wait()


def tail_lanes(slots):
    return MAIN if slots * TAIL <= MAIN else WIDE


def shards(traces, surface_point, gather_index):
    shots, receivers, samples = traces.shape
    vmem = lambda *shape, dtype=BF16: pltpu.VMEM(shape, dtype)
    hbm, anywhere = pl.BlockSpec(memory_space=pltpu.HBM), pl.BlockSpec(memory_space=pl.ANY)
    message = lambda lanes: vmem(OWNERS, PART, lanes)
    table = dft_rows(samples)
    back = [
        jax.ShapeDtypeStruct((OWNERS, SHOTS, PART, MAIN), BF16),
        jax.ShapeDtypeStruct((OWNERS, PART, WIDE), BF16),
    ]
    product = lambda slots: pl.pallas_call(
        functools.partial(kernel, slots),
        out_shape=back,
        in_specs=[hbm] * 4,
        out_specs=[anywhere, anywhere],
        scratch_shapes=[
            pltpu.SMEM((4, 2, 4), jnp.int32),
            pltpu.SMEM((4, 2, 4), jnp.int32),
            vmem(SHOTS, MAIN, dtype=jnp.int32),
            pltpu.SMEM((SHOTS, MAIN), jnp.int32),
            vmem(2 * F, samples),
            vmem(SHOTS, SHARE // PART, PART, samples),
            vmem(SHOTS, receivers // PART, PART, samples),
            vmem(SHOTS * HALF, samples),
            vmem(OWNERS, slots, PART, MAIN),
            message(MAIN),
            message(tail_lanes(slots)),
            vmem(OWNERS, slots, PART, MAIN),
            message(MAIN),
            message(MAIN),
            message(tail_lanes(slots)),
            vmem(2, OWNERS * PART, MAIN, dtype=F32),
            vmem(BINS, WIDE, 2 * WIDE),
            vmem(POINTS * PART, MAIN, dtype=F32),
            vmem(2, POINTS * PART, MAIN, dtype=F32),
            vmem(OWNERS * SHOTS * PART, MAIN, dtype=F32),
            vmem(2, OWNERS * PART, MAIN, dtype=F32),
            vmem(OWNERS, SHOTS, PART, MAIN),
            message(WIDE),
            pltpu.SemaphoreType.DMA((9,)),
            pltpu.SemaphoreType.DMA((2,)),
            pltpu.SemaphoreType.DMA((5,)),
            pltpu.SemaphoreType.DMA((5,)),
        ],
        compiler_params=pltpu.CompilerParams(
            collective_id=slots // 2, has_side_effects=True, vmem_limit_bytes=50 * 2**20
        ),
    )
    points, gathers = surface_point.transpose(0, 2, 1), gather_index.transpose(0, 2, 1)
    blocks = traces.reshape(shots, receivers // PART, PART, samples)
    case = pl.pallas_call(
        choose,
        out_shape=jax.ShapeDtypeStruct((1,), jnp.int32),
        in_specs=[pl.BlockSpec(memory_space=pltpu.SMEM)],
        out_specs=pl.BlockSpec(memory_space=pltpu.SMEM),
    )(gathers)[0]
    spectra = lax.switch(case, [product(room) for room in ROOMS], points, gathers, blocks, jnp.asarray(table))
    return pl.pallas_call(
        inverse,
        out_shape=jax.ShapeDtypeStruct((shots, SHARE, samples), BF16),
        in_specs=[pl.BlockSpec(memory_space=pltpu.VMEM)] * 3,
        out_specs=anywhere,
        scratch_shapes=[
            vmem(SHOTS, SHARE, samples),
            pltpu.SemaphoreType.DMA((SHOTS // 2,)),
        ],
        compiler_params=pltpu.CompilerParams(vmem_limit_bytes=50 * 2**20),
    )(*spectra, jnp.asarray(table[:, : samples // 2]))


def solution(mesh):
    placed = (P("shot", None, None), P(), P())
    return jax.shard_map(
        shards, mesh=mesh, in_specs=placed, out_specs=P("shot", "surf", None), check_vma=False
    )
```

```python
import functools
import math

import jax
import jax.numpy as jnp
import ml_dtypes
import numpy as np
from jax import lax
from jax.experimental import pallas as pl
from jax.experimental.pallas import tpu as pltpu
from jax.sharding import PartitionSpec as P

F = 256
OWNERS = 32
BINS = F // OWNERS
PART = 2 * BINS
SHOTS = 8
POINTS = 32
MAIN, TAIL = 128, 32
SHARE = MAIN + TAIL
HALF = POINTS // 2
WIDE = SHOTS * TAIL
MESH = pl.DeviceIdType.MESH
ROOMS = (4, 6, 8)
F32, BF16 = jnp.float32, jnp.bfloat16


def dft_rows(samples):
    freq = np.arange(F).reshape(OWNERS // 2, BINS, 2).transpose(2, 0, 1).reshape(OWNERS, 1, BINS, 1)
    angles = (freq * np.arange(samples) % samples) * (2.0 * math.pi / samples)
    table = np.concatenate([np.cos(angles), -np.sin(angles)], axis=1)
    table = table.astype(np.float32).astype(ml_dtypes.bfloat16).astype(np.float32)
    scaled = table.reshape(2 * F, samples) * samples**-0.5
    return scaled.astype(ml_dtypes.bfloat16)


def offsets():
    steps = [(z, x, y) for z in range(2) for x in range(4) for y in range(4)][1:]
    return sorted(steps, key=lambda k: -(k[0] + min(k[1], 4 - k[1]) + min(k[2], 4 - k[2])))


def wide_rows(ref, rows):
    return jnp.concatenate([ref[half, rows, :] for half in range(2)], axis=1)


def dot(a, b, contract):
    return lax.dot_general(a, b, (contract, ((), ())), preferred_element_type=F32)


def iota(shape, axis):
    return lax.broadcasted_iota(jnp.int32, shape, axis)


def product(left, right):
    real, imag = right
    both = jnp.concatenate(
        [jnp.concatenate([real, imag], axis=1), jnp.concatenate([-imag, real], axis=1)], axis=0
    )
    return dot(left, both, ((1,), (0,)))


def kernel(
    slots,
    point_ref, gather_ref, traces, table, hm, ht,
    points, gathers, slot_v, slot_of, tab, block, full, xn, sm, sn, st, rm, rn, other, rt,
    near, lhs, far_main, far_tail, om, ot, bm, bt,
    load_sem, pair_sem, send_sem, recv_sem,
):
    group, me = lax.axis_index("surf"), lax.axis_index("shot")
    core = group % 2
    z, x, y = me // 16, (me // 4) % 4, me % 4
    peers = [(z ^ k) * 16 + (x + i) % 4 * 4 + (y + j) % 4 for k, i, j in offsets()]
    away = lambda d: [n for n, step in enumerate(offsets()) if sum(map(bool, step)) == d]
    everyone = sorted(range(len(peers)), key=lambda n: (n * 12) % 31)
    groups = lax.axis_size("surf")

    share = SHARE // PART
    blocks = [pl.ds((group + k) % groups * share, share) for k in range(groups)]
    loads = [
        pltpu.make_async_copy(table, tab, load_sem.at[0]),
        pltpu.make_async_copy(traces.at[:, blocks[0]], block, load_sem.at[1]),
    ]
    for k in range(1, groups):
        part = traces.at[:, blocks[k]], full.at[:, blocks[k]]
        loads.append(pltpu.make_async_copy(*part, load_sem.at[1 + k]))
    loads.append(pltpu.make_async_copy(point_ref, points, load_sem.at[5]))
    loads.append(pltpu.make_async_copy(gather_ref, gathers, load_sem.at[6]))
    for load in loads[:2] + loads[5:]:
        load.start()
    barrier = pltpu.get_barrier_semaphore()
    pl.semaphore_signal(barrier, inc=1, device_id=(group ^ 1, me), device_id_type=MESH)
    for n in everyone:
        pl.semaphore_signal(barrier, inc=1, device_id=(group, peers[n]), device_id_type=MESH)
    for load in loads[2:5]:
        load.start()

    def start(way):
        kind, source, target = way
        pltpu.make_async_copy(source(me), target(me), recv_sem.at[kind]).start()
        for n in everyone:
            pltpu.make_async_remote_copy(
                src_ref=source(peers[n]),
                dst_ref=target(me),
                send_sem=send_sem.at[kind],
                recv_sem=recv_sem.at[kind],
                device_id=(group, peers[n]),
                device_id_type=MESH,
            ).start()

    def arrive(kind, whole):
        pltpu.make_async_copy(whole, whole, recv_sem.at[kind]).wait()

    def sent(kind, whole):
        others = whole.at[pl.ds(0, OWNERS - 1)]
        pltpu.make_async_copy(others, others, send_sem.at[kind]).wait()

    def forward(rows):
        spectra = dot(tab[...], rows, ((1,), (1,))).astype(BF16)
        return spectra.reshape(OWNERS, PART, -1)

    slot = lambda ref: lambda device: ref.at[device]
    two = lambda ref, k: lambda device: ref.at[device, pl.ds(2 * k, 2)]
    rounds = range(slots // 2)
    early = 0 if slots == ROOMS[0] else 1
    pairs = range(SHOTS // 2)
    tail_way, near_way = (0, slot(st), slot(rt)), (1, slot(sn), slot(rn))
    main_ways = [(2, two(sm, k), two(rm, k)) for k in rounds]

    for load in loads[5:]:
        load.wait()
    index = lambda i: gathers[i // 8, i // 4 % 2, i % 4]
    owner = lambda i: lax.div(index(i), SHOTS)
    if slots < SHOTS:
        wanted = wanted_of(index)
        before = jnp.zeros((1, MAIN), jnp.int32)
        for l in range(SHOTS):
            row = wanted[l : l + 1]
            slot_v[l : l + 1] = before + SHOTS * row
            before = before + row
        table_copy = pltpu.make_async_copy(slot_v, slot_of, load_sem.at[7])
        table_copy.start()
        table_copy.wait()
        mine = [0] * SHOTS
        for l in range(SHOTS):
            for k in range(slots):
                mine[k] = jnp.where(slot_of[l, me] == SHOTS + k, l, mine[k])
        place = lambda i: slot_of[lax.rem(index(i), SHOTS), owner(i)] - SHOTS
    else:
        mine = range(SHOTS)
        place = lambda i: lax.rem(index(i), SHOTS)

    loads[0].wait()
    loads[1].wait()
    spread_own = pltpu.make_async_copy(block, full.at[:, blocks[0]], load_sem.at[8])
    spread_own.start()
    main, tail = pl.ds(0, MAIN // PART), pl.ds(MAIN // PART, TAIL // PART)
    tails = st.shape[2] // TAIL
    rows = [block[mine[k], tail].reshape(TAIL, -1) for k in range(tails)]
    st[...] = forward(jnp.concatenate(rows, axis=0))
    for k in rounds:
        rows = [block[mine[2 * k + j], main].reshape(MAIN, -1) for j in range(2)]
        spectra = forward(jnp.concatenate(rows, axis=0))
        sm[:, 2 * k] = spectra[..., :MAIN]
        sm[:, 2 * k + 1] = spectra[..., MAIN:]

    pl.semaphore_wait(barrier, len(everyone) + 1)
    for way in (tail_way, *main_ways[:early]):
        start(way)

    for load in (*loads[2:5], spread_own):
        load.wait()
    chosen = jnp.zeros((HALF, 1), jnp.int32)
    aligned = []
    for i in range(HALF):
        point = points[core * 2 + i // 8, i // 4 % 2, i % 4]
        aligned.append(lax.div(point, PART))
        chosen = jnp.where(iota((HALF, 1), 0) == i, i * PART + lax.rem(point, PART), chosen)
    pick = (iota((HALF, HALF * PART), 1) == chosen).astype(BF16)
    for s in range(SHOTS):
        rows = jnp.concatenate([full[s, row] for row in aligned], axis=0)
        xn[s * HALF : (s + 1) * HALF, :] = dot(pick, rows, ((1,), (0,))).astype(BF16)
    sn[...] = forward(xn[...])
    for way in (near_way, *main_ways[early:]):
        start(way)

    lines = [[pl.ds(part * BINS + b, OWNERS, stride=PART) for part in range(2)] for b in range(BINS)]
    slot_at = iota((PART, st.shape[2]), 1) // TAIL
    wide = (st.shape[2], WIDE)
    spread = (iota(wide, 0) % TAIL == iota(wide, 1) % TAIL).astype(BF16)
    shot_of_point = lambda axis: iota((WIDE, WIDE), axis) % MAIN // HALF
    tile = lambda a: jnp.concatenate([a[:HALF]] * SHOTS + [a[HALF:]] * SHOTS, axis=0)

    arrive(0, rt)
    picked = []
    for i in range(POINTS):
        picked.append(rt[owner(i)] * (slot_at == place(i)).astype(BF16))
    spectra = dot(jnp.concatenate(picked, axis=0), spread, ((1,), (0,)))
    for half in range(2):
        far_tail[half] = spectra[:, half * MAIN : (half + 1) * MAIN]
    arrive(1, rn)
    swap = pltpu.make_async_remote_copy(
        src_ref=rn,
        dst_ref=other,
        send_sem=pair_sem.at[0],
        recv_sem=pair_sem.at[1],
        device_id=(group ^ 1, me),
        device_id_type=MESH,
    )
    swap.start()
    near[core] = rn[...].reshape(OWNERS * PART, MAIN).astype(F32)
    swap.wait()
    near[1 - core] = other[...].reshape(OWNERS * PART, MAIN).astype(F32)
    diagonal = (shot_of_point(0) == iota((WIDE, WIDE), 1) // TAIL).astype(BF16)
    for b in range(BINS):
        left = jnp.concatenate([wide_rows(near, r).astype(BF16) for r in lines[b]], axis=1)
        right = [tile(wide_rows(far_tail, r).astype(BF16)) * diagonal for r in lines[b]]
        total = -product(left, right)
        for part in range(2):
            for half in range(2):
                lanes = slice(part * WIDE + half * MAIN, part * WIDE + (half + 1) * MAIN)
                ot[half, lines[b][part], :] = total[:, lanes]
    for half in range(2):
        lanes = slice(half * MAIN, (half + 1) * MAIN)
        bt[:, :, lanes] = ot[half].reshape(OWNERS, PART, MAIN).astype(BF16)
    back_tail = 3, slot(bt), slot(ht)
    start(back_tail)
    diagonal = (iota((WIDE, WIDE), 0) // OWNERS == shot_of_point(1)).astype(BF16)
    for b in range(BINS):
        for part, r in enumerate(lines[b]):
            copies = [wide_rows(near, r).astype(BF16)] * SHOTS
            lhs[b, :, part * WIDE : (part + 1) * WIDE] = jnp.concatenate(copies, axis=0) * diagonal

    arrive(2, rm)
    for i in range(POINTS):
        far_main[i * PART : (i + 1) * PART, :] = rm[owner(i), place(i)].astype(F32)
    for b in range(BINS):
        total = -product(lhs[b], [tile(far_main[r, :].astype(BF16)) for r in lines[b]])
        for s in range(SHOTS):
            for part in range(2):
                om[pl.ds(s * PART + part * BINS + b, OWNERS, stride=SHOTS * PART), :] = total[
                    s * OWNERS : (s + 1) * OWNERS, part * MAIN : (part + 1) * MAIN
                ]
    totals = om[...].reshape(OWNERS, SHOTS, PART, MAIN)
    four = lambda ref, k: lambda device: ref.at[device, pl.ds(4 * k, 4)]
    for k in range(2):
        bm[:, 4 * k : 4 * k + 4] = totals[:, 4 * k : 4 * k + 4].astype(BF16)
        back_main = 4, four(bm, k), four(hm, k)
        start(back_main)
    arrive(3, ht)
    arrive(4, hm)
    for kind, whole in enumerate((st, sn, sm, bt, bm)):
        sent(kind, whole)


def wanted_of(index):
    gather = iota((SHOTS, MAIN), 1) * SHOTS + iota((SHOTS, MAIN), 0)
    wanted = jnp.zeros((SHOTS, MAIN), jnp.int32)
    for i in range(POINTS):
        wanted = jnp.where(gather == index(i), 1, wanted)
    return wanted


def choose(gathers, case):
    wanted = wanted_of(lambda i: gathers[i // 8, i // 4 % 2, i % 4])
    most = jnp.max(jnp.sum(wanted, axis=0, keepdims=True))
    case[0] = sum((most > room).astype(jnp.int32) for room in ROOMS[:-1])


def inverse(hm, ht, tab, out, series, store_sem):
    shots, _, samples = out.shape
    pairs = range(shots // 2)
    def invert(spectra, two, receivers):
        even = dot(spectra[:F], tab[:F], ((0,), (0,)))
        odd = dot(spectra[F:], tab[F:], ((0,), (0,)))
        shape = (two.stop - two.start, receivers.stop - receivers.start, samples // 2)
        series[two, receivers, : samples // 2] = (even + odd).astype(BF16).reshape(shape)
        series[two, receivers, samples // 2 :] = (even - odd).astype(BF16).reshape(shape)

    invert(ht[...].reshape(2 * F, WIDE), slice(0, shots), slice(MAIN, SHARE))
    stores = []
    for k in pairs:
        two = pl.ds(2 * k, 2)
        spectra = [hm[:, 2 * k + s].reshape(2 * F, MAIN) for s in range(2)]
        invert(jnp.concatenate(spectra, axis=1), slice(2 * k, 2 * k + 2), slice(0, MAIN))
        stores.append(pltpu.make_async_copy(series.at[two], out.at[two], store_sem.at[k]))
        stores[-1].start()
    for store in stores:
        store.wait()


def tail_lanes(slots):
    return MAIN if slots * TAIL <= MAIN else WIDE


def shards(traces, surface_point, gather_index):
    shots, receivers, samples = traces.shape
    vmem = lambda *shape, dtype=BF16: pltpu.VMEM(shape, dtype)
    hbm, anywhere = pl.BlockSpec(memory_space=pltpu.HBM), pl.BlockSpec(memory_space=pl.ANY)
    message = lambda lanes: vmem(OWNERS, PART, lanes)
    table = dft_rows(samples)
    back = [
        jax.ShapeDtypeStruct((OWNERS, SHOTS, PART, MAIN), BF16),
        jax.ShapeDtypeStruct((OWNERS, PART, WIDE), BF16),
    ]
    product = lambda slots: pl.pallas_call(
        functools.partial(kernel, slots),
        out_shape=back,
        in_specs=[hbm] * 4,
        out_specs=[anywhere, anywhere],
        scratch_shapes=[
            pltpu.SMEM((4, 2, 4), jnp.int32),
            pltpu.SMEM((4, 2, 4), jnp.int32),
            vmem(SHOTS, MAIN, dtype=jnp.int32),
            pltpu.SMEM((SHOTS, MAIN), jnp.int32),
            vmem(2 * F, samples),
            vmem(SHOTS, SHARE // PART, PART, samples),
            vmem(SHOTS, receivers // PART, PART, samples),
            vmem(SHOTS * HALF, samples),
            vmem(OWNERS, slots, PART, MAIN),
            message(MAIN),
            message(tail_lanes(slots)),
            vmem(OWNERS, slots, PART, MAIN),
            message(MAIN),
            message(MAIN),
            message(tail_lanes(slots)),
            vmem(2, OWNERS * PART, MAIN, dtype=F32),
            vmem(BINS, WIDE, 2 * WIDE),
            vmem(POINTS * PART, MAIN, dtype=F32),
            vmem(2, POINTS * PART, MAIN, dtype=F32),
            vmem(OWNERS * SHOTS * PART, MAIN, dtype=F32),
            vmem(2, OWNERS * PART, MAIN, dtype=F32),
            vmem(OWNERS, SHOTS, PART, MAIN),
            message(WIDE),
            pltpu.SemaphoreType.DMA((9,)),
            pltpu.SemaphoreType.DMA((2,)),
            pltpu.SemaphoreType.DMA((5,)),
            pltpu.SemaphoreType.DMA((5,)),
        ],
        compiler_params=pltpu.CompilerParams(
            collective_id=slots // 2, has_side_effects=True, vmem_limit_bytes=50 * 2**20
        ),
    )
    points, gathers = surface_point.transpose(0, 2, 1), gather_index.transpose(0, 2, 1)
    blocks = traces.reshape(shots, receivers // PART, PART, samples)
    case = pl.pallas_call(
        choose,
        out_shape=jax.ShapeDtypeStruct((1,), jnp.int32),
        in_specs=[pl.BlockSpec(memory_space=pltpu.SMEM)],
        out_specs=pl.BlockSpec(memory_space=pltpu.SMEM),
    )(gathers)[0]
    spectra = lax.switch(case, [product(room) for room in ROOMS], points, gathers, blocks, jnp.asarray(table))
    return pl.pallas_call(
        inverse,
        out_shape=jax.ShapeDtypeStruct((shots, SHARE, samples), BF16),
        in_specs=[pl.BlockSpec(memory_space=pltpu.VMEM)] * 3,
        out_specs=anywhere,
        scratch_shapes=[
            vmem(SHOTS, SHARE, samples),
            pltpu.SemaphoreType.DMA((SHOTS // 2,)),
        ],
        compiler_params=pltpu.CompilerParams(vmem_limit_bytes=50 * 2**20),
    )(*spectra, jnp.asarray(table[:, : samples // 2]))


def solution(mesh):
    placed = (P("shot", None, None), P(), P())
    return jax.shard_map(
        shards, mesh=mesh, in_specs=placed, out_specs=P("shot", "surf", None), check_vma=False
    )
```

```python
import functools
import math

import jax
import jax.numpy as jnp
import ml_dtypes
import numpy as np
from jax import lax
from jax.experimental import pallas as pl
from jax.experimental.pallas import tpu as pltpu
from jax.sharding import PartitionSpec as P

F = 256
OWNERS = 32
BINS = F // OWNERS
PART = 2 * BINS
SHOTS = 8
POINTS = 32
MAIN, TAIL = 128, 32
SHARE = MAIN + TAIL
HALF = POINTS // 2
WIDE = SHOTS * TAIL
MESH = pl.DeviceIdType.MESH
ROOMS = (4, 6, 8)
F32, BF16 = jnp.float32, jnp.bfloat16


def dft_rows(samples):
    freq = np.arange(F).reshape(OWNERS // 2, BINS, 2).transpose(2, 0, 1).reshape(OWNERS, 1, BINS, 1)
    angles = (freq * np.arange(samples) % samples) * (2.0 * math.pi / samples)
    table = np.concatenate([np.cos(angles), -np.sin(angles)], axis=1)
    table = table.astype(np.float32).astype(ml_dtypes.bfloat16).astype(np.float32)
    scaled = table.reshape(2 * F, samples) * samples**-0.5
    return scaled.astype(ml_dtypes.bfloat16)


def offsets():
    steps = [(z, x, y) for z in range(2) for x in range(4) for y in range(4)][1:]
    return sorted(steps, key=lambda k: -(k[0] + min(k[1], 4 - k[1]) + min(k[2], 4 - k[2])))


def wide_rows(ref, rows):
    return jnp.concatenate([ref[half, rows, :] for half in range(2)], axis=1)


def dot(a, b, contract):
    return lax.dot_general(a, b, (contract, ((), ())), preferred_element_type=F32)


def iota(shape, axis):
    return lax.broadcasted_iota(jnp.int32, shape, axis)


def product(left, right):
    real, imag = right
    both = jnp.concatenate(
        [jnp.concatenate([real, imag], axis=1), jnp.concatenate([-imag, real], axis=1)], axis=0
    )
    return dot(left, both, ((1,), (0,)))


def kernel(
    slots,
    point_ref, gather_ref, traces, table, hm, ht,
    points, gathers, slot_v, slot_of, tab, block, full, xn, sm, sn, st, rm, rn, other, rt,
    near, lhs, far_main, far_tail, om, ot, bm, bt,
    load_sem, pair_sem, send_sem, recv_sem,
):
    group, me = lax.axis_index("surf"), lax.axis_index("shot")
    core = group % 2
    z, x, y = me // 16, (me // 4) % 4, me % 4
    peers = [(z ^ k) * 16 + (x + i) % 4 * 4 + (y + j) % 4 for k, i, j in offsets()]
    away = lambda d: [n for n, step in enumerate(offsets()) if sum(map(bool, step)) == d]
    everyone = sorted(range(len(peers)), key=lambda n: (n * 12) % 31)
    groups = lax.axis_size("surf")

    share = SHARE // PART
    blocks = [pl.ds((group + k) % groups * share, share) for k in range(groups)]
    loads = [
        pltpu.make_async_copy(table, tab, load_sem.at[0]),
        pltpu.make_async_copy(traces.at[:, blocks[0]], block, load_sem.at[1]),
    ]
    for k in range(1, groups):
        part = traces.at[:, blocks[k]], full.at[:, blocks[k]]
        loads.append(pltpu.make_async_copy(*part, load_sem.at[1 + k]))
    loads.append(pltpu.make_async_copy(point_ref, points, load_sem.at[5]))
    loads.append(pltpu.make_async_copy(gather_ref, gathers, load_sem.at[6]))
    for load in loads[:2] + loads[5:]:
        load.start()
    barrier = pltpu.get_barrier_semaphore()
    pl.semaphore_signal(barrier, inc=1, device_id=(group ^ 1, me), device_id_type=MESH)
    for n in everyone:
        pl.semaphore_signal(barrier, inc=1, device_id=(group, peers[n]), device_id_type=MESH)
    for load in loads[2:5]:
        load.start()

    def start(way, order=everyone):
        kind, source, target = way
        pltpu.make_async_copy(source(me), target(me), recv_sem.at[kind]).start()
        for n in order:
            pltpu.make_async_remote_copy(
                src_ref=source(peers[n]),
                dst_ref=target(me),
                send_sem=send_sem.at[kind],
                recv_sem=recv_sem.at[kind],
                device_id=(group, peers[n]),
                device_id_type=MESH,
            ).start()

    def arrive(kind, whole):
        pltpu.make_async_copy(whole, whole, recv_sem.at[kind]).wait()

    def sent(kind, whole):
        others = whole.at[pl.ds(0, OWNERS - 1)]
        pltpu.make_async_copy(others, others, send_sem.at[kind]).wait()

    def forward(rows):
        spectra = dot(tab[...], rows, ((1,), (1,))).astype(BF16)
        return spectra.reshape(OWNERS, PART, -1)

    slot = lambda ref: lambda device: ref.at[device]
    two = lambda ref, k: lambda device: ref.at[device, pl.ds(2 * k, 2)]
    rounds = range(slots // 2)
    early = 0 if slots == ROOMS[0] else 1
    pairs = range(SHOTS // 2)
    tail_way, near_way = (0, slot(st), slot(rt)), (1, slot(sn), slot(rn))
    main_ways = [(2, two(sm, k), two(rm, k)) for k in rounds]

    for load in loads[5:]:
        load.wait()
    index = lambda i: gathers[i // 8, i // 4 % 2, i % 4]
    owner = lambda i: lax.div(index(i), SHOTS)
    if slots < SHOTS:
        wanted = wanted_of(index)
        before = jnp.zeros((1, MAIN), jnp.int32)
        for l in range(SHOTS):
            row = wanted[l : l + 1]
            slot_v[l : l + 1] = before + SHOTS * row
            before = before + row
        table_copy = pltpu.make_async_copy(slot_v, slot_of, load_sem.at[7])
        table_copy.start()
        table_copy.wait()
        mine = [0] * SHOTS
        for l in range(SHOTS):
            for k in range(slots):
                mine[k] = jnp.where(slot_of[l, me] == SHOTS + k, l, mine[k])
        place = lambda i: slot_of[lax.rem(index(i), SHOTS), owner(i)] - SHOTS
    else:
        mine = range(SHOTS)
        place = lambda i: lax.rem(index(i), SHOTS)

    loads[0].wait()
    loads[1].wait()
    spread_own = pltpu.make_async_copy(block, full.at[:, blocks[0]], load_sem.at[8])
    spread_own.start()
    main, tail = pl.ds(0, MAIN // PART), pl.ds(MAIN // PART, TAIL // PART)
    tails = st.shape[2] // TAIL
    rows = [block[mine[k], tail].reshape(TAIL, -1) for k in range(tails)]
    st[...] = forward(jnp.concatenate(rows, axis=0))
    for k in rounds:
        rows = [block[mine[2 * k + j], main].reshape(MAIN, -1) for j in range(2)]
        spectra = forward(jnp.concatenate(rows, axis=0))
        sm[:, 2 * k] = spectra[..., :MAIN]
        sm[:, 2 * k + 1] = spectra[..., MAIN:]

    pl.semaphore_wait(barrier, len(everyone) + 1)
    for way in (tail_way, *main_ways[:early]):
        start(way)

    for load in (*loads[2:5], spread_own):
        load.wait()
    chosen = jnp.zeros((HALF, 1), jnp.int32)
    aligned = []
    for i in range(HALF):
        point = points[core * 2 + i // 8, i // 4 % 2, i % 4]
        aligned.append(lax.div(point, PART))
        chosen = jnp.where(iota((HALF, 1), 0) == i, i * PART + lax.rem(point, PART), chosen)
    pick = (iota((HALF, HALF * PART), 1) == chosen).astype(BF16)
    for s in range(SHOTS):
        rows = jnp.concatenate([full[s, row] for row in aligned], axis=0)
        xn[s * HALF : (s + 1) * HALF, :] = dot(pick, rows, ((1,), (0,))).astype(BF16)
    sn[...] = forward(xn[...])
    for way in (near_way, *main_ways[early:]):
        start(way)

    lines = [[pl.ds(part * BINS + b, OWNERS, stride=PART) for part in range(2)] for b in range(BINS)]
    slot_at = iota((PART, st.shape[2]), 1) // TAIL
    wide = (st.shape[2], WIDE)
    spread = (iota(wide, 0) % TAIL == iota(wide, 1) % TAIL).astype(BF16)
    shot_of_point = lambda axis: iota((WIDE, WIDE), axis) % MAIN // HALF
    tile = lambda a: jnp.concatenate([a[:HALF]] * SHOTS + [a[HALF:]] * SHOTS, axis=0)

    arrive(0, rt)
    picked = []
    for i in range(POINTS):
        picked.append(rt[owner(i)] * (slot_at == place(i)).astype(BF16))
    spectra = dot(jnp.concatenate(picked, axis=0), spread, ((1,), (0,)))
    for half in range(2):
        far_tail[half] = spectra[:, half * MAIN : (half + 1) * MAIN]
    arrive(1, rn)
    swap = pltpu.make_async_remote_copy(
        src_ref=rn,
        dst_ref=other,
        send_sem=pair_sem.at[0],
        recv_sem=pair_sem.at[1],
        device_id=(group ^ 1, me),
        device_id_type=MESH,
    )
    swap.start()
    near[core] = rn[...].reshape(OWNERS * PART, MAIN).astype(F32)
    swap.wait()
    near[1 - core] = other[...].reshape(OWNERS * PART, MAIN).astype(F32)
    diagonal = (shot_of_point(0) == iota((WIDE, WIDE), 1) // TAIL).astype(BF16)
    for b in range(BINS):
        left = jnp.concatenate([wide_rows(near, r).astype(BF16) for r in lines[b]], axis=1)
        right = [tile(wide_rows(far_tail, r).astype(BF16)) * diagonal for r in lines[b]]
        total = -product(left, right)
        for part in range(2):
            for half in range(2):
                lanes = slice(part * WIDE + half * MAIN, part * WIDE + (half + 1) * MAIN)
                ot[half, lines[b][part], :] = total[:, lanes]
    for half in range(2):
        lanes = slice(half * MAIN, (half + 1) * MAIN)
        bt[:, :, lanes] = ot[half].reshape(OWNERS, PART, MAIN).astype(BF16)
    back_tail = 3, slot(bt), slot(ht)
    start(back_tail)
    diagonal = (iota((WIDE, WIDE), 0) // OWNERS == shot_of_point(1)).astype(BF16)
    for b in range(BINS):
        for part, r in enumerate(lines[b]):
            copies = [wide_rows(near, r).astype(BF16)] * SHOTS
            lhs[b, :, part * WIDE : (part + 1) * WIDE] = jnp.concatenate(copies, axis=0) * diagonal

    arrive(2, rm)
    for i in range(POINTS):
        far_main[i * PART : (i + 1) * PART, :] = rm[owner(i), place(i)].astype(F32)
    for b in range(BINS):
        total = -product(lhs[b], [tile(far_main[r, :].astype(BF16)) for r in lines[b]])
        for s in range(SHOTS):
            for part in range(2):
                om[pl.ds(s * PART + part * BINS + b, OWNERS, stride=SHOTS * PART), :] = total[
                    s * OWNERS : (s + 1) * OWNERS, part * MAIN : (part + 1) * MAIN
                ]
    totals = om[...].reshape(OWNERS, SHOTS, PART, MAIN)
    four = lambda ref, k: lambda device: ref.at[device, pl.ds(4 * k, 4)]
    for k in range(2):
        bm[:, 4 * k : 4 * k + 4] = totals[:, 4 * k : 4 * k + 4].astype(BF16)
        back_main = 4, four(bm, k), four(hm, k)
        start(back_main, everyone[16 * k :] + everyone[: 16 * k])
    arrive(3, ht)
    arrive(4, hm)
    for kind, whole in enumerate((st, sn, sm, bt, bm)):
        sent(kind, whole)


def wanted_of(index):
    gather = iota((SHOTS, MAIN), 1) * SHOTS + iota((SHOTS, MAIN), 0)
    wanted = jnp.zeros((SHOTS, MAIN), jnp.int32)
    for i in range(POINTS):
        wanted = jnp.where(gather == index(i), 1, wanted)
    return wanted


def choose(gathers, case):
    wanted = wanted_of(lambda i: gathers[i // 8, i // 4 % 2, i % 4])
    most = jnp.max(jnp.sum(wanted, axis=0, keepdims=True))
    case[0] = sum((most > room).astype(jnp.int32) for room in ROOMS[:-1])


def inverse(hm, ht, tab, out, series, store_sem):
    shots, _, samples = out.shape
    pairs = range(shots // 2)
    def invert(spectra, two, receivers):
        even = dot(spectra[:F], tab[:F], ((0,), (0,)))
        odd = dot(spectra[F:], tab[F:], ((0,), (0,)))
        shape = (two.stop - two.start, receivers.stop - receivers.start, samples // 2)
        series[two, receivers, : samples // 2] = (even + odd).astype(BF16).reshape(shape)
        series[two, receivers, samples // 2 :] = (even - odd).astype(BF16).reshape(shape)

    invert(ht[...].reshape(2 * F, WIDE), slice(0, shots), slice(MAIN, SHARE))
    stores = []
    for k in pairs:
        two = pl.ds(2 * k, 2)
        spectra = [hm[:, 2 * k + s].reshape(2 * F, MAIN) for s in range(2)]
        invert(jnp.concatenate(spectra, axis=1), slice(2 * k, 2 * k + 2), slice(0, MAIN))
        stores.append(pltpu.make_async_copy(series.at[two], out.at[two], store_sem.at[k]))
        stores[-1].start()
    for store in stores:
        store.wait()


def tail_lanes(slots):
    return MAIN if slots * TAIL <= MAIN else WIDE


def shards(traces, surface_point, gather_index):
    shots, receivers, samples = traces.shape
    vmem = lambda *shape, dtype=BF16: pltpu.VMEM(shape, dtype)
    hbm, anywhere = pl.BlockSpec(memory_space=pltpu.HBM), pl.BlockSpec(memory_space=pl.ANY)
    message = lambda lanes: vmem(OWNERS, PART, lanes)
    table = dft_rows(samples)
    back = [
        jax.ShapeDtypeStruct((OWNERS, SHOTS, PART, MAIN), BF16),
        jax.ShapeDtypeStruct((OWNERS, PART, WIDE), BF16),
    ]
    product = lambda slots: pl.pallas_call(
        functools.partial(kernel, slots),
        out_shape=back,
        in_specs=[hbm] * 4,
        out_specs=[anywhere, anywhere],
        scratch_shapes=[
            pltpu.SMEM((4, 2, 4), jnp.int32),
            pltpu.SMEM((4, 2, 4), jnp.int32),
            vmem(SHOTS, MAIN, dtype=jnp.int32),
            pltpu.SMEM((SHOTS, MAIN), jnp.int32),
            vmem(2 * F, samples),
            vmem(SHOTS, SHARE // PART, PART, samples),
            vmem(SHOTS, receivers // PART, PART, samples),
            vmem(SHOTS * HALF, samples),
            vmem(OWNERS, slots, PART, MAIN),
            message(MAIN),
            message(tail_lanes(slots)),
            vmem(OWNERS, slots, PART, MAIN),
            message(MAIN),
            message(MAIN),
            message(tail_lanes(slots)),
            vmem(2, OWNERS * PART, MAIN, dtype=F32),
            vmem(BINS, WIDE, 2 * WIDE),
            vmem(POINTS * PART, MAIN, dtype=F32),
            vmem(2, POINTS * PART, MAIN, dtype=F32),
            vmem(OWNERS * SHOTS * PART, MAIN, dtype=F32),
            vmem(2, OWNERS * PART, MAIN, dtype=F32),
            vmem(OWNERS, SHOTS, PART, MAIN),
            message(WIDE),
            pltpu.SemaphoreType.DMA((9,)),
            pltpu.SemaphoreType.DMA((2,)),
            pltpu.SemaphoreType.DMA((5,)),
            pltpu.SemaphoreType.DMA((5,)),
        ],
        compiler_params=pltpu.CompilerParams(
            collective_id=slots // 2, has_side_effects=True, vmem_limit_bytes=50 * 2**20
        ),
    )
    points, gathers = surface_point.transpose(0, 2, 1), gather_index.transpose(0, 2, 1)
    blocks = traces.reshape(shots, receivers // PART, PART, samples)
    case = pl.pallas_call(
        choose,
        out_shape=jax.ShapeDtypeStruct((1,), jnp.int32),
        in_specs=[pl.BlockSpec(memory_space=pltpu.SMEM)],
        out_specs=pl.BlockSpec(memory_space=pltpu.SMEM),
    )(gathers)[0]
    spectra = lax.switch(case, [product(room) for room in ROOMS], points, gathers, blocks, jnp.asarray(table))
    return pl.pallas_call(
        inverse,
        out_shape=jax.ShapeDtypeStruct((shots, SHARE, samples), BF16),
        in_specs=[pl.BlockSpec(memory_space=pltpu.VMEM)] * 3,
        out_specs=anywhere,
        scratch_shapes=[
            vmem(SHOTS, SHARE, samples),
            pltpu.SemaphoreType.DMA((SHOTS // 2,)),
        ],
        compiler_params=pltpu.CompilerParams(vmem_limit_bytes=50 * 2**20),
    )(*spectra, jnp.asarray(table[:, : samples // 2]))


def solution(mesh):
    placed = (P("shot", None, None), P(), P())
    return jax.shard_map(
        shards, mesh=mesh, in_specs=placed, out_specs=P("shot", "surf", None), check_vma=False
    )
```
